32 devices in a mesh: tower: 2 (over x), crops: 16 (over z, y, core).
Axes of the slice: x: 2, y: 2, z: 4, core: 2. Of those that a mesh axis runs over, the one named last changes fastest.
Arguments:
- features: bfloat16 [2, 2048, 13, 13, 384], P('tower', 'crops'), may hold values from -6 to 6
- conv_weight: bfloat16 [2, 3, 3, 384, 256], P('tower'), may hold values from -0.109375 to 0.109375
- conv_bias: float32 [2, 256], P('tower'), may hold values from -3 to 3
- fc_weight: bfloat16 [2, 9216, 4096], P('tower', 'crops'), may hold values from -0.0625 to 0.0625
- fc_bias: float32 [2, 4096], P('tower'), may hold values from -3 to 3
- stitch_pool: float32 [2, 2, 256], P('tower'), may hold values from 0.2 to 1
- stitch_fc: float32 [2, 2, 4096], P('tower'), may hold values from 0.2 to 1
- cotangent: bfloat16 [2, 2048, 4096], P('tower', 'crops'), may hold values from -6 to 6
- crop_counts: int32 [512], P('crops'), may hold values from 1 to 4
- slot_image: int32 [2048], P('crops'), may hold values from 0 to 31, as said below
- slot_mask: int32 [2048], P('crops'), may hold values from 0 to 1, as said below
Outputs:
- output: bfloat16 [2, 2048, 4096], P('tower', 'crops')
- grad_features: bfloat16 [2, 2048, 13, 13, 384], P('tower', 'crops')
- grad_conv_weight: float32 [2, 3, 3, 384, 256], P('tower')
- grad_conv_bias: float32 [2, 256], P('tower')
- grad_fc_weight: float32 [2, 9216, 4096], P('tower', 'crops')
- grad_fc_bias: float32 [2, 4096], P('tower')
- grad_stitch_pool: float32 [2, 2, 256], P('tower')
- grad_stitch_fc: float32 [2, 2, 4096], P('tower')
The draws below stay inside these ranges and needn't reach their ends.
Inputs may be any that keep to these rules, and one draw needn't show every extreme that they name: Within each device's 128 slots the numbers never fall; slot_image names one of that device's 32 images, and the first and last slot of each device name images 0 and 31. `slot_mask`: each device's live slots come first; every device has at least 64 live slots, and in every draw some device has all 128 live.
All inputs are finite; a program needn't handle non-finite values.
Results may differ from the reference program's by a relative error of at most 0.0082.
Values may be sent and summed in bfloat16 or wider, within the bound.
No kernel may reach another device: no remote copies, remote signals or barrier semaphores. Data moves between devices by JAX's collectives and lax.ppermute only.
A program may use at most 704 MiB of HBM per device.

```python
import jax
import jax.numpy as jnp
from jax import lax

C4 = 384
C5 = 256
HID = 4096
SIDE = 13
SLOTS = 128
FLAT = 9216
IMG_DEV = 32
CROPS = 2048
IMAGES = 512
N_TOWER = 2
N_CROPS = 16


def draw_slot_image(key, part):
    key = jax.random.fold_in(key, 11)
    raw_ids = jax.random.randint(key, (N_CROPS, SLOTS), 0, IMG_DEV)
    raw_ids = raw_ids.at[:, 0].set(0).at[:, SLOTS - 1].set(IMG_DEV - 1)
    return jnp.sort(raw_ids, axis=1).reshape(CROPS).astype(jnp.int32)


def draw_slot_mask(key, part):
    key = jax.random.fold_in(key, 23)
    key_live, key_full = jax.random.split(key)
    live_count = jax.random.randint(key_live, (N_CROPS,), SLOTS // 2, SLOTS + 1)
    full_device = jax.random.randint(key_full, (), 0, N_CROPS)
    live_count = jnp.where(jnp.arange(N_CROPS) == full_device, SLOTS, live_count)
    filled = jnp.arange(SLOTS)[None, :] < live_count[:, None]
    return filled.astype(jnp.int32).reshape(CROPS)


def set_ends(drawn, own_key, least, high):
    shape = drawn.shape
    spot = [jax.random.randint(jax.random.fold_in(own_key, axis), (), 0, shape[axis]) for axis in range(len(shape))]
    drawn = drawn.at[tuple(spot)].set(least)
    longest = shape.index(max(shape))
    spot[longest] = (spot[longest] + 1) % shape[longest]
    return drawn.at[tuple(spot)].set(high)


def shard_levels(stream_key, shape, shards, smallest, high):
    def one(axis_at, shards_of):
        heights = jax.random.uniform(jax.random.fold_in(jax.random.fold_in(stream_key, 6), axis_at), (shards_of,), jnp.float32, smallest / len(shards), high / len(shards))
        return jnp.repeat(jnp.exp(heights), shape[axis_at] // shards_of).reshape((-1,) + (1,) * (len(shape) - axis_at - 1))

    gain = one(*shards[0])
    for cut in shards[1:]:
        gain = gain * one(*cut)
    return gain


def normal_values(own_key, dims, deviation, bound, cuts=(), dtype=jnp.bfloat16):
    level = shard_levels(own_key, dims, cuts, -0.22, 0.18) if cuts else 1.0
    drawn = jax.random.normal(own_key, dims, jnp.float32) * deviation * level
    return jnp.minimum(jnp.maximum(drawn, -bound), bound).astype(dtype)


def setup_inputs(seed: int = 0) -> dict:
    key_of = jax.random.split(jax.random.key(seed), 12)
    features = normal_values(key_of[0], (N_TOWER, CROPS, SIDE, SIDE, C4), 1.0, 6.0, ((0, 2), (1, 16)))
    conv_weight = normal_values(key_of[1], (N_TOWER, 3, 3, C4, C5), (9 * C4) ** -0.5, 0.109375, ((0, 2),))
    conv_bias = normal_values(key_of[2], (N_TOWER, C5), 0.5, 3.0, ((0, 2),), jnp.float32)
    fc_weight = normal_values(key_of[3], (N_TOWER, FLAT, HID), FLAT ** -0.5, 0.0625, ((0, 2), (1, 16)))
    fc_bias = normal_values(key_of[4], (N_TOWER, HID), 0.5, 3.0, ((0, 2),), jnp.float32)
    stitch_pool = jnp.clip(0.2 + 0.8 * jax.random.uniform(key_of[5], (N_TOWER, 2, C5), jnp.float32) ** shard_levels(key_of[5], (N_TOWER, 2, C5), ((0, 2),), -0.2, 0.2), 0.2, 1.0)
    stitch_fc = jnp.clip(0.2 + 0.8 * jax.random.uniform(key_of[6], (N_TOWER, 2, HID), jnp.float32) ** shard_levels(key_of[6], (N_TOWER, 2, HID), ((0, 2),), -0.2, 0.2), 0.2, 1.0)
    cotangent = normal_values(key_of[7], (N_TOWER, CROPS, HID), 1.0, 6.0, ((0, 2), (1, 16)))
    crop_counts = set_ends(jax.random.randint(key_of[8], (IMAGES,), 1, 5), jax.random.fold_in(key_of[8], 1), 1, 4).astype(jnp.int32)
    slot_image = draw_slot_image(jax.random.fold_in(key_of[11], 71), 0)
    slot_mask = draw_slot_mask(jax.random.fold_in(key_of[11], 71), 0)
    return dict(features=features, conv_weight=conv_weight, conv_bias=conv_bias, fc_weight=fc_weight, fc_bias=fc_bias, stitch_pool=stitch_pool, stitch_fc=stitch_fc, cotangent=cotangent, crop_counts=crop_counts, slot_image=slot_image, slot_mask=slot_mask)


@jax.custom_vjp
def low(v):
    return lax.optimization_barrier(v.astype(jnp.bfloat16)).astype(jnp.float32)

@jax.custom_vjp
def low_back(v):
    return v

def low_keep(v):
    return (low(v), None)

def low_pass(kept, grad):
    return (grad,)

def back_keep(v):
    return (v, None)

def back_low(kept, grad):
    return (low(grad),)
low.defvjp(low_keep, low_pass)
low_back.defvjp(back_keep, back_low)

def smooth_gelu(argument):
    return jax.nn.gelu(argument, approximate=True)

def smooth_pool(activity):
    extent = activity.shape[1]
    stride_span = 2 * ((extent - 3) // 2 + 1) - 1
    summed = jnp.zeros((activity.shape[0], (extent - 3) // 2 + 1, (extent - 3) // 2 + 1, activity.shape[3]), jnp.float32)
    for row_shift in range(3):
        for col_shift in range(3):
            window = activity[:, row_shift:row_shift + stride_span:2, col_shift:col_shift + stride_span:2, :]
            summed = summed + jnp.exp(window)
    return jnp.log(summed)

def conv_apply(inputs, kernel):
    extent = inputs.shape[1]
    padded = jnp.pad(inputs, ((0, 0), (1, 1), (1, 1), (0, 0)))
    summed = jnp.zeros(inputs.shape[:3] + (kernel.shape[3],), jnp.float32)
    for row_shift in range(3):
        for col_shift in range(3):
            window = padded[:, row_shift:row_shift + extent, col_shift:col_shift + extent, :]
            summed = summed + jnp.einsum('bhwc,cd->bhwd', window, kernel[row_shift, col_shift], precision=lax.Precision.HIGHEST)
    return summed

def forward(params, inputs):
    conv_weight, conv_bias, fc_weight, fc_bias, stitch_pool, stitch_fc = params
    pooled = []
    for tower_id in range(2):
        pre_conv = low_back(conv_apply(inputs[tower_id], conv_weight[tower_id]) + conv_bias[tower_id])
        pooled.append(low(smooth_pool(smooth_gelu(pre_conv))))
    hidden = []
    for tower_id in range(2):
        partner = 1 - tower_id
        mixed = stitch_pool[tower_id, tower_id] * pooled[tower_id] + stitch_pool[tower_id, partner] * low_back(pooled[partner])
        mixed = low(mixed.reshape(mixed.shape[0], -1))
        pre_fc = low_back(jnp.dot(mixed, fc_weight[tower_id], precision=lax.Precision.HIGHEST) + fc_bias[tower_id])
        hidden.append(low(smooth_gelu(pre_fc)))
    stitched = []
    for tower_id in range(2):
        partner = 1 - tower_id
        stitched.append(stitch_fc[tower_id, tower_id] * hidden[tower_id] + stitch_fc[tower_id, partner] * low_back(hidden[partner]))
    return jnp.stack(stitched)

def reference(features, conv_weight, conv_bias, fc_weight, fc_bias, stitch_pool, stitch_fc, cotangent, crop_counts, slot_image, slot_mask):
    params = (conv_weight.astype(jnp.float32), conv_bias.astype(jnp.float32), fc_weight.astype(jnp.float32), fc_bias.astype(jnp.float32), stitch_pool.astype(jnp.float32), stitch_fc.astype(jnp.float32))
    counts_dev = crop_counts.reshape(N_CROPS, IMG_DEV)
    images_dev = slot_image.reshape(N_CROPS, SLOTS)
    masks_dev = slot_mask.reshape(N_CROPS, SLOTS)
    feature_blocks = jnp.moveaxis(features.reshape(2, N_CROPS, SLOTS, SIDE, SIDE, C4), 1, 0)
    cotangent_blocks = jnp.moveaxis(cotangent.reshape(2, N_CROPS, SLOTS, HID), 1, 0)

    def scan_step(running, blocks_in):
        feature_blk, cotangent_blk, count_blk, image_blk, mask_blk = blocks_in
        live_slots = mask_blk.astype(jnp.float32)
        per_slot = count_blk.astype(jnp.float32)[image_blk.astype(jnp.int32)]
        scaling = live_slots / per_slot
        result, pullback = jax.vjp(forward, params, feature_blk.astype(jnp.float32))
        grad_params, grad_inputs = pullback(cotangent_blk.astype(jnp.float32) * scaling[None, :, None])
        running = jax.tree.map(jnp.add, running, grad_params)
        shown = (result * live_slots[None, :, None]).astype(jnp.bfloat16)
        return (running, (shown, grad_inputs.astype(jnp.bfloat16)))
    zero_grads = jax.tree.map(jnp.zeros_like, params)
    grad_sums, (outputs_all, grad_blocks) = lax.scan(scan_step, zero_grads, (feature_blocks, cotangent_blocks, counts_dev, images_dev, masks_dev))
    output = jnp.moveaxis(outputs_all, 0, 1).reshape(2, CROPS, HID)
    grad_features = jnp.moveaxis(grad_blocks, 0, 1).reshape(2, CROPS, SIDE, SIDE, C4)
    return (output, grad_features, grad_sums[0], grad_sums[1], grad_sums[2], grad_sums[3], grad_sums[4], grad_sums[5])
```

```python
import functools

import jax
import jax.numpy as jnp
from jax import lax
from jax.experimental import pallas as pl
from jax.experimental.pallas import tpu as pltpu
from jax.sharding import PartitionSpec as P

CHUNKS = 4
BF16 = jnp.bfloat16
F32 = jnp.float32
CONV_DIMS = ("NHWC", "HWIO", "NHWC")
VMEM_LIMIT = 48 * 1024 * 1024


def swap_crops(block, mask):
    count = lax.axis_size("crops")
    return lax.ppermute(block, "crops", [(i, i ^ mask) for i in range(count)])


def swap_tower(block):
    return lax.ppermute(block, "tower", [(0, 1), (1, 0)])


def pick(stack, index):
    return lax.dynamic_index_in_dim(stack, index, 0, keepdims=False)


def pool_kernel(e_ref, pooled_ref, inv_ref):
    extent = e_ref.shape[0]
    width = e_ref.shape[3]
    out = (extent - 3) // 2 + 1

    def columns(row):
        cells = [e_ref[row, col].astype(F32) for col in range(extent)]
        return [cells[2 * j] + cells[2 * j + 1] + cells[2 * j + 2] for j in range(out)]

    top = columns(0)
    for i in range(out):
        middle = columns(2 * i + 1)
        bottom = columns(2 * i + 2)
        for j in range(out):
            total = top[j] + middle[j] + bottom[j]
            lanes = pl.ds((i * out + j) * width, width)
            pooled_ref[:, lanes] = jnp.log(total).astype(pooled_ref.dtype)
            inv_ref[:, lanes] = 2.0 / total
        top = bottom


def pool_forward(e):
    extent, _, slots, width = e.shape
    out = (extent - 3) // 2 + 1
    block = 16
    flat = out * out * width
    return pl.pallas_call(
        pool_kernel,
        grid=(slots // block,),
        in_specs=[pl.BlockSpec((extent, extent, block, width), lambda s: (0, 0, s, 0))],
        out_specs=[
            pl.BlockSpec((block, flat), lambda s: (s, 0)),
            pl.BlockSpec((block, flat), lambda s: (s, 0)),
        ],
        out_shape=[
            jax.ShapeDtypeStruct((slots, flat), BF16),
            jax.ShapeDtypeStruct((slots, flat), F32),
        ],
        compiler_params=pltpu.CompilerParams(vmem_limit_bytes=VMEM_LIMIT),
        cost_estimate=pl.CostEstimate(
            flops=4 * e.size, bytes_accessed=2 * e.size + 6 * slots * flat, transcendentals=0
        ),
        name="pool_forward",
    )(e)


def pool_back_kernel(slope_ref, grad_ref, back_ref, inv_ref, self_ref, g_ref, bias_ref):
    extent = slope_ref.shape[0]
    width = slope_ref.shape[3]
    out = (extent - 3) // 2 + 1
    coef = self_ref[0:1, :]

    @pl.when(pl.program_id(0) == 0)
    def _():
        bias_ref[...] = jnp.zeros_like(bias_ref)

    def window_row(i):
        row = []
        for j in range(out):
            lanes = pl.ds((i * out + j) * width, width)
            grad = coef * grad_ref[:, lanes].astype(F32) + back_ref[:, lanes].astype(F32)
            row.append(grad * inv_ref[:, lanes])
        return row

    sums = jnp.zeros((slope_ref.shape[2], width), F32)
    above = None
    current = window_row(0)
    for row in range(extent):
        if row % 2 == 0:
            if row == 0:
                rows = current
            elif row == extent - 1:
                rows = current
            else:
                above, current = current, window_row(row // 2)
                rows = [a + b for a, b in zip(above, current)]
        else:
            rows = current
        for col in range(extent):
            if col % 2 == 1:
                spread = rows[col // 2]
            elif col == 0:
                spread = rows[0]
            elif col == extent - 1:
                spread = rows[out - 1]
            else:
                spread = rows[col // 2 - 1] + rows[col // 2]
            grad = (slope_ref[row, col].astype(F32) * spread).astype(g_ref.dtype)
            g_ref[row, col] = grad
            sums = sums + grad.astype(F32)
    bias_ref[...] += sums


def pool_backward(slope, grad_mixed, back_pool, inv, self_pool):
    extent, _, slots, width = slope.shape
    block = 16
    flat = grad_mixed.shape[1]
    rows = pl.BlockSpec((block, flat), lambda s: (s, 0))
    grid_block = pl.BlockSpec((extent, extent, block, width), lambda s: (0, 0, s, 0))
    return pl.pallas_call(
        pool_back_kernel,
        grid=(slots // block,),
        in_specs=[grid_block, rows, rows, rows, pl.BlockSpec((1, width), lambda s: (0, 0))],
        out_specs=[grid_block, pl.BlockSpec((block, width), lambda s: (0, 0))],
        out_shape=[
            jax.ShapeDtypeStruct(slope.shape, BF16),
            jax.ShapeDtypeStruct((block, width), F32),
        ],
        compiler_params=pltpu.CompilerParams(vmem_limit_bytes=VMEM_LIMIT),
        cost_estimate=pl.CostEstimate(
            flops=4 * slope.size, bytes_accessed=4 * slope.size + 8 * slots * flat, transcendentals=0
        ),
        name="pool_backward",
    )(slope, grad_mixed, back_pool, inv, self_pool[None])


def gelu_parts(v):
    root = 0.7978845608028654
    cubic = 0.044715
    tanh = jnp.tanh(root * (v + cubic * (v * v * v)))
    half = 0.5 * (1.0 + tanh)
    slope = half + 0.5 * v * (1.0 - tanh * tanh) * (root * (1.0 + 3.0 * cubic * (v * v)))
    return v * half, slope


def conv_forward(inputs, kernel, bias):
    pre_conv = lax.conv_general_dilated(
        inputs, kernel, (1, 1), ((1, 1), (1, 1)), dimension_numbers=CONV_DIMS, preferred_element_type=F32
    )
    activity, slope = gelu_parts(pre_conv + bias)
    e = jnp.exp(activity)
    return e.astype(BF16), ((0.5 * e) * slope).astype(BF16)


def conv_grad_inputs(grad_pre, kernel):
    turned = jnp.flip(kernel, (0, 1)).swapaxes(2, 3)
    return lax.conv_general_dilated(
        grad_pre, turned, (1, 1), ((1, 1), (1, 1)), dimension_numbers=CONV_DIMS, preferred_element_type=F32
    ).astype(BF16)


def conv_grad_kernel(inputs, grad_pre):
    dims = lax.ConvDimensionNumbers(lhs_spec=(3, 0, 1, 2), rhs_spec=(3, 0, 1, 2), out_spec=(2, 3, 0, 1))
    return lax.conv_general_dilated(
        inputs, grad_pre, (1, 1), ((1, 1), (1, 1)), dimension_numbers=dims, preferred_element_type=F32
    )


def sum_small(vector):
    step = 1
    while step < lax.axis_size("crops"):
        vector = vector + swap_crops(vector, step)
        step *= 2
    return vector


def sum_kernel(rows, outer, mid, core):
    width = rows.shape[1]
    outer_count = lax.axis_size("crops") // 4
    for mask, side in ((1, core), (2, mid)):
        halves = rows.reshape(2, -1, width)
        got = swap_crops(pick(halves, 1 - side).astype(BF16), mask)
        rows = pick(halves, side) + got.astype(F32)
    parts = rows.reshape(outer_count, -1, width)
    total = pick(parts, outer)
    for k in range(1, outer_count):
        total = total + swap_crops(pick(parts, outer ^ k).astype(BF16), 4 * k).astype(F32)
    total = total.astype(BF16)
    stack = jnp.stack([total] + [swap_crops(total, 4 * k) for k in range(1, outer_count)])
    rows = jnp.concatenate([pick(stack, outer ^ k) for k in range(outer_count)])
    for mask, side in ((2, mid), (1, core)):
        got = swap_crops(rows, mask)
        rows = jnp.where(side == 0, jnp.concatenate([rows, got]), jnp.concatenate([got, rows]))
    return rows.astype(F32)


def body(
    features,
    conv_weight,
    conv_bias,
    fc_weight,
    fc_bias,
    stitch_pool,
    stitch_fc,
    cotangent,
    crop_counts,
    slot_image,
    slot_mask,
):
    is_first = lax.axis_index("tower") == 0
    place = lax.axis_index("crops")
    core, mid, outer = place & 1, (place >> 1) & 1, place >> 2
    outer_count = lax.axis_size("crops") // 4
    own_rows = fc_weight[0]
    other_rows = swap_crops(own_rows, 2)
    block = own_rows.shape[0]
    units = own_rows.shape[1]

    row_pool = stitch_pool[0]
    self_pool = jnp.where(is_first, row_pool[0], row_pool[1])
    cross_pool = jnp.where(is_first, row_pool[1], row_pool[0])
    row_fc = stitch_fc[0]
    self_fc = jnp.where(is_first, row_fc[0], row_fc[1])
    cross_fc = jnp.where(is_first, row_fc[1], row_fc[0])

    live_slots = slot_mask.astype(F32)
    image_ids = jnp.arange(crop_counts.shape[0], dtype=jnp.int32)
    matches = (slot_image[:, None] == image_ids[None, :]).astype(F32)
    per_slot = jnp.sum(matches * crop_counts.astype(F32)[None, :], axis=1)
    scaling = live_slots / per_slot
    sent_fc = (cross_fc * (cotangent[0].astype(F32) * scaling[:, None])).astype(BF16)
    back_fc = swap_tower(sent_fc)

    inputs = features[0]
    kernel = conv_weight[0]
    slots = inputs.shape[0] // CHUNKS
    width = kernel.shape[3]
    cells = outer_count * 4 * block // width
    self_flat = jnp.tile(self_pool, cells)
    cross_flat = jnp.tile(cross_pool, cells)

    def column_block(array, o, m, c):
        start = ((o * 2 + m) * 2 + c) * block
        return array[:, start : start + block]

    def spread_rows(mixed):
        keep, give = [], []
        for o in range(outer_count):
            parts = [[column_block(mixed, o, m, c) for c in range(2)] for m in range(2)]
            own = [jnp.where(mid == 0, parts[0][c], parts[1][c]) for c in range(2)]
            far = [jnp.where(mid == 0, parts[1][c], parts[0][c]) for c in range(2)]
            keep.append(
                jnp.concatenate([jnp.where(core == 0, own[0], own[1]), jnp.where(core == 0, far[0], far[1])], axis=1)
            )
            give.append(
                jnp.concatenate([jnp.where(core == 0, own[1], own[0]), jnp.where(core == 0, far[1], far[0])], axis=1)
            )
        got = swap_crops(jnp.stack(give), 1)
        blocks = jnp.stack([jnp.stack(keep), got], axis=1)
        arrived = [pick(blocks, outer)]
        for k in range(1, outer_count):
            arrived.append(swap_crops(pick(blocks, outer ^ k), 4 * k))
        return jnp.stack(arrived)

    def join_rows(columns):
        arrived = [columns[0]] + [swap_crops(columns[k], 4 * k) for k in range(1, outer_count)]
        stack = jnp.stack(arrived)
        own_core = stack[:, 0]
        far_core = swap_crops(stack[:, 1], 1)
        pieces = []
        for o in range(outer_count):
            here, there = pick(own_core, outer ^ o), pick(far_core, outer ^ o)
            by_core = [jnp.where(core == 0, here, there), jnp.where(core == 0, there, here)]
            for m in range(2):
                for c in range(2):
                    first, second = by_core[c][:, :block], by_core[c][:, block:]
                    pieces.append(jnp.where(mid == m, first, second))
        return jnp.concatenate(pieces, axis=1)

    outputs, grads_in = [], []
    hidden_self = hidden_cross = fc_bias_sum = 0.0
    pool_self = pool_cross = conv_bias_sum = 0.0
    kernel_sum = 0.0
    stage = []
    for n in range(CHUNKS):
        part = inputs[n * slots : (n + 1) * slots]
        e, slope = conv_forward(part, kernel, conv_bias[0])
        pooled, inv = pool_forward(jnp.transpose(e, (1, 2, 0, 3)))
        partner_pool = swap_tower(pooled)
        mixed = (self_flat * pooled.astype(F32) + cross_flat * partner_pool.astype(F32)).astype(BF16)
        columns = spread_rows(mixed)
        flat = columns.reshape(-1, 2 * block)
        partial = jnp.dot(flat[:, :block], own_rows, preferred_element_type=F32) + jnp.dot(
            flat[:, block:], other_rows, preferred_element_type=F32
        )
        partial = partial.astype(BF16).reshape(outer_count, 2, slots, units)
        chip = (partial[:, 0].astype(F32) + swap_crops(partial[:, 1], 1).astype(F32)).astype(BF16)
        pre_fc = chip[0].astype(F32)
        for k in range(1, outer_count):
            pre_fc = pre_fc + swap_crops(chip[k], 4 * k).astype(F32)
        pre_fc = pre_fc + fc_bias[0]
        hidden, slope_fc = gelu_parts(pre_fc)
        hidden = hidden.astype(BF16)
        rows = slice(n * slots, (n + 1) * slots)
        grad_out = cotangent[0][rows].astype(F32) * scaling[rows, None]
        grad_pre_fc = ((self_fc * grad_out + back_fc[rows].astype(F32)) * slope_fc).astype(BF16)
        fc_bias_sum = fc_bias_sum + jnp.sum(grad_pre_fc.astype(F32), axis=0)
        around = jnp.stack([grad_pre_fc] + [swap_crops(grad_pre_fc, 4 * k) for k in range(1, outer_count)])
        gathered = jnp.stack([around, swap_crops(around, 1)], axis=1).reshape(-1, units)
        turned = (((1,), (1,)), ((), ()))
        grad_columns = jnp.concatenate(
            [
                lax.dot_general(gathered, own_rows, turned, preferred_element_type=F32).astype(BF16),
                lax.dot_general(gathered, other_rows, turned, preferred_element_type=F32).astype(BF16),
            ],
            axis=1,
        )
        grad_mixed = join_rows(grad_columns.reshape(outer_count, 2, slots, 2 * block))
        wide = grad_mixed.astype(F32)
        pool_self = pool_self + jnp.sum(pooled.astype(F32) * wide, axis=0)
        pool_cross = pool_cross + jnp.sum(partner_pool.astype(F32) * wide, axis=0)
        back_pool = swap_tower((cross_flat * wide).astype(BF16))
        grad_pre, bias_rows = pool_backward(
            jnp.transpose(slope, (1, 2, 0, 3)), grad_mixed, back_pool, inv, self_pool
        )
        conv_bias_sum = conv_bias_sum + jnp.sum(bias_rows, axis=0)
        grad_pre = jnp.transpose(grad_pre, (2, 0, 1, 3))
        kernel_sum = kernel_sum + conv_grad_kernel(part, grad_pre)
        grads_in.append(conv_grad_inputs(grad_pre, kernel))
        partner_hidden = swap_tower(hidden)
        stitched = self_fc * hidden.astype(F32) + cross_fc * partner_hidden.astype(F32)
        outputs.append((stitched * live_slots[rows, None]).astype(BF16))
        hidden_self = hidden_self + jnp.sum(hidden.astype(F32) * grad_out, axis=0)
        hidden_cross = hidden_cross + jnp.sum(partner_hidden.astype(F32) * grad_out, axis=0)
        stage.append((flat, gathered))

    all_columns = jnp.concatenate([s[0] for s in stage])
    all_grads = jnp.concatenate([s[1] for s in stage])
    lead = (((0,), (0,)), ((), ()))
    far_term = lax.dot_general(all_columns[:, block:], all_grads, lead, preferred_element_type=F32).astype(BF16)
    grad_fc_weight = lax.dot_general(
        all_columns[:, :block], all_grads, lead, preferred_element_type=F32
    ) + swap_crops(far_term, 2).astype(F32)

    pool_self = jnp.sum(pool_self.reshape(cells, width), axis=0)
    pool_cross = jnp.sum(pool_cross.reshape(cells, width), axis=0)
    small = sum_small(
        jnp.concatenate([conv_bias_sum, pool_self, pool_cross, fc_bias_sum, hidden_self, hidden_cross])[None]
    )[0]
    cuts = [width, 2 * width, 3 * width, 3 * width + units, 3 * width + 2 * units]
    conv_bias_sum, pool_self, pool_cross, fc_bias_sum, hidden_self, hidden_cross = jnp.split(small, cuts)
    grad_row_pool = jnp.where(
        is_first, jnp.stack([pool_self, pool_cross]), jnp.stack([pool_cross, pool_self])
    )
    grad_row_fc = jnp.where(
        is_first, jnp.stack([hidden_self, hidden_cross]), jnp.stack([hidden_cross, hidden_self])
    )
    summed_kernel = sum_kernel(kernel_sum.reshape(-1, width), outer, mid, core).reshape(kernel.shape)
    return (
        jnp.concatenate(outputs)[None],
        jnp.concatenate(grads_in)[None],
        summed_kernel[None],
        conv_bias_sum[None],
        grad_fc_weight[None],
        fc_bias_sum[None],
        grad_row_pool[None],
        grad_row_fc[None],
    )


def solution(mesh):
    placed = (
        P("tower", "crops", None, None, None),
        P("tower", None, None, None, None),
        P("tower", None),
        P("tower", "crops", None),
        P("tower", None),
        P("tower", None, None),
        P("tower", None, None),
        P("tower", "crops", None),
        P("crops"),
        P("crops"),
        P("crops"),
    )
    return jax.shard_map(
        body,
        mesh=mesh,
        in_specs=placed,
        out_specs=(
            P("tower", "crops", None),
            P("tower", "crops", None, None, None),
            P("tower", None, None, None, None),
            P("tower", None),
            P("tower", "crops", None),
            P("tower", None),
            P("tower", None, None),
            P("tower", None, None),
        ),
        check_vma=False,
    )
```

```python
import functools

import jax
import jax.numpy as jnp
from jax import lax
from jax.experimental import pallas as pl
from jax.experimental.pallas import tpu as pltpu
from jax.sharding import PartitionSpec as P

PLAN = "01020130120321301223013201320103211030212130232W132303123W"
BF16 = jnp.bfloat16
F32 = jnp.float32
CONV_DIMS = ("NHWC", "HWIO", "NHWC")
VMEM_LIMIT = 48 * 1024 * 1024


def swap_core(block):
    return lax.ppermute(block, "core", [(0, 1), (1, 0)])


def swap_mid(block):
    return lax.ppermute(block, "mid", [(0, 1), (1, 0)])


def swap_outer(block, mask):
    count = lax.axis_size("outer")
    return lax.ppermute(block, "outer", [(i, i ^ mask) for i in range(count)])


def swap_tower(block):
    return lax.ppermute(block, "tower", [(0, 1), (1, 0)])


def pick(stack, index):
    return lax.dynamic_index_in_dim(stack, index, 0, keepdims=False)


def pool_kernel(e_ref, pooled_ref, inv_ref):
    extent = e_ref.shape[0]
    width = e_ref.shape[3]
    out = (extent - 3) // 2 + 1

    def columns(row):
        cells = [e_ref[row, col].astype(F32) for col in range(extent)]
        return [cells[2 * j] + cells[2 * j + 1] + cells[2 * j + 2] for j in range(out)]

    top = columns(0)
    for i in range(out):
        middle = columns(2 * i + 1)
        bottom = columns(2 * i + 2)
        for j in range(out):
            total = top[j] + middle[j] + bottom[j]
            lanes = pl.ds((i * out + j) * width, width)
            pooled_ref[:, lanes] = jnp.log(total).astype(pooled_ref.dtype)
            inv_ref[:, lanes] = 2.0 / total
        top = bottom


def pool_forward(e):
    extent, _, slots, width = e.shape
    out = (extent - 3) // 2 + 1
    block = 16
    flat = out * out * width
    return pl.pallas_call(
        pool_kernel,
        grid=(slots // block,),
        in_specs=[pl.BlockSpec((extent, extent, block, width), lambda s: (0, 0, s, 0))],
        out_specs=[
            pl.BlockSpec((block, flat), lambda s: (s, 0)),
            pl.BlockSpec((block, flat), lambda s: (s, 0)),
        ],
        out_shape=[
            jax.ShapeDtypeStruct((slots, flat), BF16),
            jax.ShapeDtypeStruct((slots, flat), F32),
        ],
        compiler_params=pltpu.CompilerParams(vmem_limit_bytes=VMEM_LIMIT),
        cost_estimate=pl.CostEstimate(flops=0, bytes_accessed=0, transcendentals=0),
        name="pool_forward",
    )(e)


def pool_back_kernel(slope_ref, grad_ref, back_ref, inv_ref, self_ref, g_ref, bias_ref):
    extent = slope_ref.shape[0]
    width = slope_ref.shape[3]
    out = (extent - 3) // 2 + 1
    coef = self_ref[0:1, :]

    @pl.when(pl.program_id(0) == 0)
    def _():
        bias_ref[...] = jnp.zeros_like(bias_ref)

    def window_row(i):
        row = []
        for j in range(out):
            lanes = pl.ds((i * out + j) * width, width)
            grad = coef * grad_ref[:, lanes].astype(F32) + back_ref[:, lanes].astype(F32)
            row.append(grad * inv_ref[:, lanes])
        return row

    sums = jnp.zeros((slope_ref.shape[2], width), F32)
    above = None
    current = window_row(0)
    for row in range(extent):
        if row % 2 == 0:
            if row == 0:
                rows = current
            elif row == extent - 1:
                rows = current
            else:
                above, current = current, window_row(row // 2)
                rows = [a + b for a, b in zip(above, current)]
        else:
            rows = current
        for col in range(extent):
            if col % 2 == 1:
                spread = rows[col // 2]
            elif col == 0:
                spread = rows[0]
            elif col == extent - 1:
                spread = rows[out - 1]
            else:
                spread = rows[col // 2 - 1] + rows[col // 2]
            grad = (slope_ref[row, col].astype(F32) * spread).astype(g_ref.dtype)
            g_ref[row, col] = grad
            sums = sums + grad.astype(F32)
    bias_ref[...] += sums


def pool_backward(slope, grad_mixed, back_pool, inv, self_pool):
    extent, _, slots, width = slope.shape
    block = 16
    flat = grad_mixed.shape[1]
    rows = pl.BlockSpec((block, flat), lambda s: (s, 0))
    grid_block = pl.BlockSpec((extent, extent, block, width), lambda s: (0, 0, s, 0))
    return pl.pallas_call(
        pool_back_kernel,
        grid=(slots // block,),
        in_specs=[grid_block, rows, rows, rows, pl.BlockSpec((1, width), lambda s: (0, 0))],
        out_specs=[grid_block, pl.BlockSpec((block, width), lambda s: (0, 0))],
        out_shape=[
            jax.ShapeDtypeStruct(slope.shape, BF16),
            jax.ShapeDtypeStruct((block, width), F32),
        ],
        compiler_params=pltpu.CompilerParams(vmem_limit_bytes=VMEM_LIMIT),
        cost_estimate=pl.CostEstimate(flops=0, bytes_accessed=0, transcendentals=0),
        name="pool_backward",
    )(slope, grad_mixed, back_pool, inv, self_pool[None])


def mix_kernel(block, target_ref, core_ref, pooled_ref, partner_ref, self_ref, cross_ref, *out_refs):
    reach = 4 * block
    is_zero = core_ref[0] == 0
    for p, out_ref in enumerate(out_refs):
        lanes = pl.ds(pl.multiple_of(target_ref[p] * reach, 128), reach)
        mixed = self_ref[...] * pooled_ref[:, lanes].astype(F32) + cross_ref[...] * partner_ref[:, lanes].astype(F32)
        piece = [mixed[:, i * block : (i + 1) * block] for i in range(4)]
        first = jnp.concatenate([piece[0], piece[2]], axis=1)
        second = jnp.concatenate([piece[1], piece[3]], axis=1)
        out_ref[0] = jnp.where(is_zero, first, second).astype(out_ref.dtype)
        out_ref[1] = jnp.where(is_zero, second, first).astype(out_ref.dtype)


def mix(pooled, partner_pool, self_pool, cross_pool, target, core, block):
    slots, flat = pooled.shape
    count = flat // (4 * block)
    shape = jax.ShapeDtypeStruct((2, slots, 2 * block), BF16)
    if (4 * block) % 128:
        width = self_pool.shape[0]
        mixed = (
            jnp.tile(self_pool, flat // width) * pooled.astype(F32)
            + jnp.tile(cross_pool, flat // width) * partner_pool.astype(F32)
        ).astype(BF16)
        mixed = mixed.reshape(slots, count, 2, 2, block).transpose(1, 3, 0, 2, 4).reshape(count, 2, slots, 2 * block)
        mixed = jnp.where(core == 0, mixed, mixed[:, ::-1])
        return [pick(mixed, target[p]) for p in range(count)]
    repeat = 4 * block // self_pool.shape[0]
    smem = pl.BlockSpec(memory_space=pltpu.SMEM)
    vmem = pl.BlockSpec(memory_space=pltpu.VMEM)
    return pl.pallas_call(
        functools.partial(mix_kernel, block),
        in_specs=[smem, smem, vmem, vmem, vmem, vmem],
        out_specs=[vmem] * count,
        out_shape=[shape] * count,
        compiler_params=pltpu.CompilerParams(vmem_limit_bytes=VMEM_LIMIT),
        cost_estimate=pl.CostEstimate(flops=0, bytes_accessed=0, transcendentals=0),
        name="mix",
    )(target, core[None], pooled, partner_pool, jnp.tile(self_pool, repeat)[None], jnp.tile(cross_pool, repeat)[None])


def join_kernel(block, count, width, target_ref, core_ref, cross_ref, pooled_ref, partner_ref, far_ref, *refs):
    here_refs = refs[:count]
    grad_ref, sent_ref, sums_ref = refs[count:]
    reach = 4 * block
    is_zero = core_ref[0] == 0
    own_sum = jnp.zeros((1, reach), F32)
    cross_sum = jnp.zeros((1, reach), F32)
    for p in range(count):
        lanes = pl.ds(pl.multiple_of(target_ref[p] * reach, 128), reach)
        here, there = here_refs[p][0].astype(F32), far_ref[p].astype(F32)
        zero, one = jnp.where(is_zero, here, there), jnp.where(is_zero, there, here)
        grad = jnp.concatenate([zero[:, :block], one[:, :block], zero[:, block:], one[:, block:]], axis=1)
        grad_ref[:, lanes] = grad.astype(grad_ref.dtype)
        sent_ref[:, lanes] = (cross_ref[...] * grad).astype(sent_ref.dtype)
        own_sum = own_sum + jnp.sum(pooled_ref[:, lanes].astype(F32) * grad, axis=0, keepdims=True)
        cross_sum = cross_sum + jnp.sum(partner_ref[:, lanes].astype(F32) * grad, axis=0, keepdims=True)
    for row, total in enumerate((own_sum, cross_sum)):
        folded = total[:, :width]
        for cell in range(1, reach // width):
            folded = folded + total[:, cell * width : (cell + 1) * width]
        sums_ref[row : row + 1, :] = folded


def join(here, far, pooled, partner_pool, cross_pool, target, core, block):
    slots, flat = pooled.shape
    count = flat // (4 * block)
    width = cross_pool.shape[0]
    if (4 * block) % 128:
        pieces = jnp.stack([jnp.stack([here[p][0], far[p]]) for p in range(count)])
        pieces = jnp.where(core == 0, pieces, pieces[:, ::-1]).reshape(count, 2, slots, 2, block)
        inverse = jnp.argsort(target)
        grad = jnp.take(pieces, inverse, axis=0).transpose(2, 0, 3, 1, 4).reshape(slots, flat)
        wide = grad.astype(F32)
        sent = (jnp.tile(cross_pool, flat // width) * wide).astype(BF16)
        sums = [
            jnp.sum(jnp.sum(a.astype(F32) * wide, axis=0).reshape(-1, width), axis=0) for a in (pooled, partner_pool)
        ]
        return grad, sent, jnp.stack(sums)
    smem = pl.BlockSpec(memory_space=pltpu.SMEM)
    vmem = pl.BlockSpec(memory_space=pltpu.VMEM)
    return pl.pallas_call(
        functools.partial(join_kernel, block, count, width),
        in_specs=[smem, smem] + [vmem] * (4 + count),
        out_specs=[vmem] * 3,
        out_shape=[
            jax.ShapeDtypeStruct((slots, flat), BF16),
            jax.ShapeDtypeStruct((slots, flat), BF16),
            jax.ShapeDtypeStruct((2, width), F32),
        ],
        compiler_params=pltpu.CompilerParams(vmem_limit_bytes=VMEM_LIMIT),
        cost_estimate=pl.CostEstimate(flops=0, bytes_accessed=0, transcendentals=0),
        name="join",
    )(target, core[None], jnp.tile(cross_pool, 4 * block // width)[None], pooled, partner_pool, far, *here)


def fc_forward_kernel(count, w_ref, got_ref, *refs):
    row_refs = refs[:count]
    chip_ref, sent_ref, all_ref = refs[count:]
    slots = got_ref.shape[1]

    @pl.when(pl.program_id(0) == 0)
    def _():
        for p in range(count):
            all_ref[pl.ds(p * slots, slots), :] = row_refs[p][0]
            all_ref[pl.ds((count + p) * slots, slots), :] = got_ref[p]

    total = jnp.dot(all_ref[...], w_ref[...], preferred_element_type=F32)
    half = count * slots
    for p in range(count):
        chip_ref[p] = total[p * slots : (p + 1) * slots]
        sent_ref[p] = total[half + p * slots : half + (p + 1) * slots].astype(sent_ref.dtype)


def fc_forward(rows, got, weight):
    count, (slots, depth), units = len(rows), got.shape[1:], weight.shape[1]
    tile = 1024
    if count > 4:
        used = jnp.concatenate([r[0] for r in rows] + [got.reshape(-1, depth)])
        total = jnp.dot(used, weight, preferred_element_type=F32).reshape(2, count, slots, units)
        return total[0], total[1].astype(BF16), used
    mine = pl.BlockSpec((1, slots, depth), lambda t: (0, 0, 0))
    out = pl.BlockSpec((count, slots, tile), lambda t: (0, 0, t))
    size = 2 * count * slots
    return pl.pallas_call(
        functools.partial(fc_forward_kernel, count),
        grid=(units // tile,),
        in_specs=[
            pl.BlockSpec((depth, tile), lambda t: (0, t)),
            pl.BlockSpec((count, slots, depth), lambda t: (0, 0, 0)),
        ]
        + [mine] * count,
        out_specs=[out, out, pl.BlockSpec((size, depth), lambda t: (0, 0))],
        out_shape=[
            jax.ShapeDtypeStruct((count, slots, units), F32),
            jax.ShapeDtypeStruct((count, slots, units), BF16),
            jax.ShapeDtypeStruct((size, depth), BF16),
        ],
        compiler_params=pltpu.CompilerParams(vmem_limit_bytes=VMEM_LIMIT),
        cost_estimate=pl.CostEstimate(flops=0, bytes_accessed=0, transcendentals=0),
        name="fc_forward",
    )(weight, got, *rows)


def fc_back_kernel(count, w_ref, own_ref, came_ref, *refs):
    slots = own_ref.shape[1]
    turned = (((1,), (1,)), ((), ()))
    for side, grads in enumerate((own_ref, came_ref)):
        rows = grads[...].reshape(count * slots, grads.shape[2])
        total = lax.dot_general(rows, w_ref[...], turned, preferred_element_type=F32)
        for p in range(count):
            refs[p][side] = total[p * slots : (p + 1) * slots].astype(refs[p].dtype)


def fc_backward(own, came, weight):
    count, slots, units = own.shape
    depth = weight.shape[0]
    tile = 384 if depth % 384 == 0 else depth
    if count > 4:
        grads = jnp.stack([own, came], axis=1).reshape(-1, units)
        columns = lax.dot_general(grads, weight, (((1,), (1,)), ((), ())), preferred_element_type=F32)
        columns = columns.astype(BF16).reshape(count, 2, slots, depth)
        return [columns[p] for p in range(count)]
    grads = pl.BlockSpec((count, slots, units), lambda t: (0, 0, 0))
    return pl.pallas_call(
        functools.partial(fc_back_kernel, count),
        grid=(depth // tile,),
        in_specs=[pl.BlockSpec((tile, units), lambda t: (t, 0)), grads, grads],
        out_specs=[pl.BlockSpec((2, slots, tile), lambda t: (0, 0, t))] * count,
        out_shape=[jax.ShapeDtypeStruct((2, slots, depth), BF16)] * count,
        compiler_params=pltpu.CompilerParams(vmem_limit_bytes=VMEM_LIMIT),
        cost_estimate=pl.CostEstimate(flops=0, bytes_accessed=0, transcendentals=0),
        name="fc_backward",
    )(weight, own, came)


def gelu_parts(v):
    root = 0.7978845608028654
    cubic = 0.044715
    tanh = jnp.tanh(root * (v + cubic * (v * v * v)))
    half = 0.5 * (1.0 + tanh)
    slope = half + 0.5 * v * (1.0 - tanh * tanh) * (root * (1.0 + 3.0 * cubic * (v * v)))
    return v * half, slope


def conv_forward(inputs, kernel, bias):
    pre_conv = lax.conv_general_dilated(
        inputs, kernel, (1, 1), ((1, 1), (1, 1)), dimension_numbers=CONV_DIMS, preferred_element_type=F32
    )
    activity, slope = gelu_parts(pre_conv + bias)
    e = jnp.exp(activity)
    return e.astype(BF16), ((0.5 * e) * slope).astype(BF16)


def conv_grad_inputs(grad_pre, kernel):
    turned = jnp.flip(kernel, (0, 1)).swapaxes(2, 3)
    return lax.conv_general_dilated(
        grad_pre, turned, (1, 1), ((1, 1), (1, 1)), dimension_numbers=CONV_DIMS, preferred_element_type=F32
    ).astype(BF16)


def conv_grad_kernel(inputs, grad_pre):
    dims = lax.ConvDimensionNumbers(lhs_spec=(3, 0, 1, 2), rhs_spec=(3, 0, 1, 2), out_spec=(2, 3, 0, 1))
    return lax.conv_general_dilated(
        inputs, grad_pre, (1, 1), ((1, 1), (1, 1)), dimension_numbers=dims, preferred_element_type=F32
    )


def sum_small(vector):
    vector = vector + swap_core(vector)
    vector = vector + swap_mid(vector)
    step = 1
    while step < lax.axis_size("outer"):
        vector = vector + swap_outer(vector, step)
        step *= 2
    return vector


def sum_kernel(rows, outer, mid, core):
    outer_count = lax.axis_size("outer")
    for swap, side in ((swap_core, core), (swap_mid, mid)):
        halves = rows.reshape(2, -1, rows.shape[1])
        got = swap(pick(halves, 1 - side).astype(BF16))
        rows = pick(halves, side) + got.astype(F32)
    parts = rows.reshape(outer_count, -1, rows.shape[1])
    total = pick(parts, outer)
    for k in range(1, outer_count):
        total = total + swap_outer(pick(parts, outer ^ k).astype(BF16), k).astype(F32)
    total = total.astype(BF16)
    stack = jnp.stack([total] + [swap_outer(total, k) for k in range(1, outer_count)])
    rows = jnp.concatenate([pick(stack, outer ^ k) for k in range(outer_count)])
    for swap, side in ((swap_mid, mid), (swap_core, core)):
        got = swap(rows)
        rows = jnp.where(side == 0, jnp.concatenate([rows, got]), jnp.concatenate([got, rows]))
    return rows.astype(F32)


def body(
    features,
    conv_weight,
    conv_bias,
    fc_weight,
    fc_bias,
    stitch_pool,
    stitch_fc,
    cotangent,
    crop_counts,
    slot_image,
    slot_mask,
):
    is_first = lax.axis_index("tower") == 0
    core, mid, outer = lax.axis_index("core"), lax.axis_index("mid"), lax.axis_index("outer")
    outer_count = lax.axis_size("outer")
    block, units = fc_weight.shape[1:]
    weight = lax.all_gather(fc_weight[0], "mid", axis=0, tiled=True)

    row_pool = stitch_pool[0]
    self_pool = jnp.where(is_first, row_pool[0], row_pool[1])
    cross_pool = jnp.where(is_first, row_pool[1], row_pool[0])
    row_fc = stitch_fc[0]
    self_fc = jnp.where(is_first, row_fc[0], row_fc[1])
    cross_fc = jnp.where(is_first, row_fc[1], row_fc[0])

    live_slots = slot_mask.astype(F32)
    image_ids = jnp.arange(crop_counts.shape[0], dtype=jnp.int32)
    matches = (slot_image[:, None] == image_ids[None, :]).astype(F32)
    per_slot = jnp.sum(matches * crop_counts.astype(F32)[None, :], axis=1)
    scaling = live_slots / per_slot
    sent_fc = (cross_fc * (cotangent[0].astype(F32) * scaling[:, None])).astype(BF16)
    back_fc = swap_tower(sent_fc)

    inputs = features[0]
    kernel = conv_weight[0]
    width = kernel.shape[3]
    hops = outer_count.bit_length() - 1
    order = [sum(((p >> b) & 1) << (hops - 1 - b) for b in range(hops)) for p in range(outer_count)]
    target = outer ^ jnp.array(order, jnp.int32)
    total_slots = inputs.shape[0]
    sizes = [total_slots // 4] * 4 if outer_count <= 4 else [total_slots]
    starts = [sum(sizes[:n]) for n in range(len(sizes))]
    last = [scaling]

    def after(array):
        return lax.optimization_barrier((array, last[0]))[0]

    sums = dict(fc_bias=0.0, hidden_self=0.0, hidden_cross=0.0, pool=0.0, conv_bias=0.0, kernel=0.0)
    stage = {}
    outputs, grads_in = {}, {}
    lead = (((0,), (0,)), ((), ()))

    def chunk(n):
        slots = sizes[n]
        rows = slice(starts[n], starts[n] + slots)
        part = inputs[rows]
        e, slope = conv_forward(part, kernel, after(conv_bias[0]))
        pooled, inv = pool_forward(jnp.transpose(e, (1, 2, 0, 3)))
        last[0] = pooled
        partner_pool = swap_tower(pooled)
        yield
        rows_of = mix(after(pooled), partner_pool, self_pool, cross_pool, target, core, block)
        last[0] = rows_of[0]
        arrived = [rows_of[0]] + [swap_outer(r, k) for r, k in zip(rows_of[1:], order[1:])]
        yield
        arrived[0] = after(arrived[0])
        give = jnp.stack([r[1] for r in arrived])
        last[0] = give
        got = swap_core(give)
        yield
        chip, sent, flat = fc_forward(arrived, after(got), weight)
        last[0] = sent
        came = swap_core(sent)
        yield
        for hop in range(hops):
            chip = chip + after(came).astype(F32)
            half = chip.shape[0] // 2
            sent = chip[half:].astype(BF16)
            chip = chip[:half]
            last[0] = sent
            came = swap_outer(sent, 1 << hop)
            yield
        pre_fc = chip[0] + after(came)[0].astype(F32) + fc_bias[0]
        hidden, slope_fc = gelu_parts(pre_fc)
        hidden = hidden.astype(BF16)
        grad_out = cotangent[0][rows].astype(F32) * scaling[rows, None]
        grad_pre_fc = ((self_fc * grad_out + back_fc[rows].astype(F32)) * slope_fc).astype(BF16)
        sums["fc_bias"] += jnp.sum(grad_pre_fc.astype(F32), axis=0)
        last[0] = grad_pre_fc
        gathered = grad_pre_fc[None]
        for hop in reversed(range(hops)):
            came = swap_outer(gathered, 1 << hop)
            if hop == hops - 1:
                partner_hidden = swap_tower(hidden)
            yield
            gathered = jnp.concatenate([gathered, after(came)])
            last[0] = gathered
        came = swap_core(gathered)
        yield
        came = after(came)
        stage[n] = (flat, gathered, came)
        columns = fc_backward(gathered, came, weight)
        last[0] = columns[0]
        arrived = [columns[0]] + [swap_outer(c, k) for c, k in zip(columns[1:], order[1:])]
        yield
        arrived[0] = after(arrived[0])
        give = jnp.stack([r[1] for r in arrived])
        last[0] = give
        far = swap_core(give)
        yield
        grad_mixed, sent, stitch_sums = join(
            arrived, after(far), pooled, partner_pool, cross_pool, target, core, block
        )
        sums["pool"] += stitch_sums
        last[0] = sent
        back_pool = swap_tower(sent)
        yield
        grad_pre, bias_rows = pool_backward(
            jnp.transpose(slope, (1, 2, 0, 3)), grad_mixed, after(back_pool), inv, self_pool
        )
        sums["conv_bias"] += jnp.sum(bias_rows, axis=0)
        grad_pre = jnp.transpose(grad_pre, (2, 0, 1, 3))
        grad_kernel = conv_grad_kernel(part, grad_pre)
        sums["kernel"] += grad_kernel
        last[0] = grad_kernel
        yield
        grads_in[n] = conv_grad_inputs(after(grad_pre), kernel)
        last[0] = grads_in[n]
        stitched = self_fc * hidden.astype(F32) + cross_fc * partner_hidden.astype(F32)
        outputs[n] = (stitched * live_slots[rows, None]).astype(BF16)
        sums["hidden_self"] += jnp.sum(hidden.astype(F32) * grad_out, axis=0)
        sums["hidden_cross"] += jnp.sum(partner_hidden.astype(F32) * grad_out, axis=0)

    def fc_weight_gradient():
        columns = jnp.concatenate([stage[n][0] for n in range(len(sizes))])
        grads = after(jnp.concatenate([g.reshape(-1, units) for n in range(len(sizes)) for g in stage[n][1:]]))
        own, far = columns[:, :block], columns[:, block:]
        own, far = jnp.where(mid == 0, own, far), jnp.where(mid == 0, far, own)
        far_term = lax.dot_general(far, grads, lead, preferred_element_type=F32).astype(BF16)
        last[0] = far_term
        came = swap_mid(far_term)
        yield
        own, came = lax.optimization_barrier((own, after(came)))
        stage["gradient"] = lax.dot_general(own, grads, lead, preferred_element_type=F32) + came.astype(F32)
        last[0] = stage["gradient"]

    running = [chunk(n) for n in range(len(sizes))]
    weight_run = fc_weight_gradient()
    for n in PLAN if len(sizes) > 1 else "0" * (2 * hops + 6) + "W" + "0" * 5 + "W":
        next(weight_run if n == "W" else running[int(n)], None)
    outputs = [outputs[n] for n in range(len(sizes))]
    grads_in = [grads_in[n] for n in range(len(sizes))]
    grad_fc_weight = stage["gradient"]
    kernel_sum = sums["kernel"]
    conv_bias_sum, fc_bias_sum = sums["conv_bias"], sums["fc_bias"]
    hidden_self, hidden_cross = sums["hidden_self"], sums["hidden_cross"]
    pool_self, pool_cross = sums["pool"]

    small = sum_small(
        jnp.concatenate([conv_bias_sum, pool_self, pool_cross, fc_bias_sum, hidden_self, hidden_cross])[None]
    )[0]
    cuts = [width, 2 * width, 3 * width, 3 * width + units, 3 * width + 2 * units]
    conv_bias_sum, pool_self, pool_cross, fc_bias_sum, hidden_self, hidden_cross = jnp.split(small, cuts)
    grad_row_pool = jnp.where(
        is_first, jnp.stack([pool_self, pool_cross]), jnp.stack([pool_cross, pool_self])
    )
    grad_row_fc = jnp.where(
        is_first, jnp.stack([hidden_self, hidden_cross]), jnp.stack([hidden_cross, hidden_self])
    )
    summed_kernel = sum_kernel(kernel_sum.reshape(-1, width), outer, mid, core).reshape(kernel.shape)
    return (
        jnp.concatenate(outputs)[None],
        jnp.concatenate(grads_in)[None],
        summed_kernel[None],
        conv_bias_sum[None],
        grad_fc_weight[None],
        fc_bias_sum[None],
        grad_row_pool[None],
        grad_row_fc[None],
    )


def solution(mesh):
    mesh = jax.sharding.Mesh(mesh.devices.reshape(mesh.shape["tower"], -1, 2, 2), ("tower", "outer", "mid", "core"))
    crops = ("outer", "mid", "core")
    placed = (
        P("tower", crops, None, None, None),
        P("tower", None, None, None, None),
        P("tower", None),
        P("tower", crops, None),
        P("tower", None),
        P("tower", None, None),
        P("tower", None, None),
        P("tower", crops, None),
        P(crops),
        P(crops),
        P(crops),
    )
    return jax.shard_map(
        body,
        mesh=mesh,
        in_specs=placed,
        out_specs=(
            P("tower", crops, None),
            P("tower", crops, None, None, None),
            P("tower", None, None, None, None),
            P("tower", None),
            P("tower", crops, None),
            P("tower", None),
            P("tower", None, None),
            P("tower", None, None),
        ),
        check_vma=False,
    )
```

```python
import functools

import jax
import jax.numpy as jnp
from jax import lax
from jax.experimental import pallas as pl
from jax.experimental.pallas import tpu as pltpu
from jax.sharding import PartitionSpec as P

PLAN = "0102010213012301320130210321301230210231S021302123W2313W32S3"
BF16 = jnp.bfloat16
F32 = jnp.float32
CONV_DIMS = ("NHWC", "HWIO", "NHWC")
VMEM_LIMIT = 48 * 1024 * 1024


def swap_core(block):
    return lax.ppermute(block, "core", [(0, 1), (1, 0)])


def swap_mid(block):
    return lax.ppermute(block, "mid", [(0, 1), (1, 0)])


def swap_outer(block, mask):
    count = lax.axis_size("outer")
    return lax.ppermute(block, "outer", [(i, i ^ mask) for i in range(count)])


def swap_tower(block):
    return lax.ppermute(block, "tower", [(0, 1), (1, 0)])


def pick(stack, index):
    return lax.dynamic_index_in_dim(stack, index, 0, keepdims=False)


def pool_kernel(e_ref, pooled_ref, inv_ref):
    extent = e_ref.shape[0]
    width = e_ref.shape[3]
    out = (extent - 3) // 2 + 1

    def columns(row):
        cells = [e_ref[row, col].astype(F32) for col in range(extent)]
        return [cells[2 * j] + cells[2 * j + 1] + cells[2 * j + 2] for j in range(out)]

    top = columns(0)
    for i in range(out):
        middle = columns(2 * i + 1)
        bottom = columns(2 * i + 2)
        for j in range(out):
            total = top[j] + middle[j] + bottom[j]
            lanes = pl.ds((i * out + j) * width, width)
            pooled_ref[:, lanes] = jnp.log(total).astype(pooled_ref.dtype)
            inv_ref[:, lanes] = 2.0 / total
        top = bottom


def pool_forward(e):
    extent, _, slots, width = e.shape
    out = (extent - 3) // 2 + 1
    block = 16
    flat = out * out * width
    return pl.pallas_call(
        pool_kernel,
        grid=(slots // block,),
        in_specs=[pl.BlockSpec((extent, extent, block, width), lambda s: (0, 0, s, 0))],
        out_specs=[
            pl.BlockSpec((block, flat), lambda s: (s, 0)),
            pl.BlockSpec((block, flat), lambda s: (s, 0)),
        ],
        out_shape=[
            jax.ShapeDtypeStruct((slots, flat), BF16),
            jax.ShapeDtypeStruct((slots, flat), F32),
        ],
        compiler_params=pltpu.CompilerParams(vmem_limit_bytes=VMEM_LIMIT),
        cost_estimate=pl.CostEstimate(flops=0, bytes_accessed=0, transcendentals=0),
        name="pool_forward",
    )(e)


def pool_back_kernel(slope_ref, grad_ref, back_ref, inv_ref, self_ref, g_ref, bias_ref):
    extent = slope_ref.shape[0]
    width = slope_ref.shape[3]
    out = (extent - 3) // 2 + 1
    coef = self_ref[0:1, :]

    @pl.when(pl.program_id(0) == 0)
    def _():
        bias_ref[...] = jnp.zeros_like(bias_ref)

    def window_row(i):
        row = []
        for j in range(out):
            lanes = pl.ds((i * out + j) * width, width)
            grad = coef * grad_ref[:, lanes].astype(F32) + back_ref[:, lanes].astype(F32)
            row.append(grad * inv_ref[:, lanes])
        return row

    sums = jnp.zeros((slope_ref.shape[2], width), F32)
    above = None
    current = window_row(0)
    for row in range(extent):
        if row % 2 == 0:
            if row == 0:
                rows = current
            elif row == extent - 1:
                rows = current
            else:
                above, current = current, window_row(row // 2)
                rows = [a + b for a, b in zip(above, current)]
        else:
            rows = current
        for col in range(extent):
            if col % 2 == 1:
                spread = rows[col // 2]
            elif col == 0:
                spread = rows[0]
            elif col == extent - 1:
                spread = rows[out - 1]
            else:
                spread = rows[col // 2 - 1] + rows[col // 2]
            grad = (slope_ref[row, col].astype(F32) * spread).astype(g_ref.dtype)
            g_ref[row, col] = grad
            sums = sums + grad.astype(F32)
    bias_ref[...] += sums


def pool_backward(slope, grad_mixed, back_pool, inv, self_pool):
    extent, _, slots, width = slope.shape
    block = 16
    flat = grad_mixed.shape[1]
    rows = pl.BlockSpec((block, flat), lambda s: (s, 0))
    grid_block = pl.BlockSpec((extent, extent, block, width), lambda s: (0, 0, s, 0))
    return pl.pallas_call(
        pool_back_kernel,
        grid=(slots // block,),
        in_specs=[grid_block, rows, rows, rows, pl.BlockSpec((1, width), lambda s: (0, 0))],
        out_specs=[grid_block, pl.BlockSpec((block, width), lambda s: (0, 0))],
        out_shape=[
            jax.ShapeDtypeStruct(slope.shape, BF16),
            jax.ShapeDtypeStruct((block, width), F32),
        ],
        compiler_params=pltpu.CompilerParams(vmem_limit_bytes=VMEM_LIMIT),
        cost_estimate=pl.CostEstimate(flops=0, bytes_accessed=0, transcendentals=0),
        name="pool_backward",
    )(slope, grad_mixed, back_pool, inv, self_pool[None])


def mix_kernel(block, target_ref, core_ref, pooled_ref, partner_ref, self_ref, cross_ref, *out_refs):
    reach = 4 * block
    is_zero = core_ref[0] == 0
    for p, out_ref in enumerate(out_refs):
        lanes = pl.ds(pl.multiple_of(target_ref[p] * reach, 128), reach)
        mixed = self_ref[...] * pooled_ref[:, lanes].astype(F32) + cross_ref[...] * partner_ref[:, lanes].astype(F32)
        first = mixed[:, : 2 * block]
        second = mixed[:, 2 * block :]
        out_ref[0] = jnp.where(is_zero, first, second).astype(out_ref.dtype)
        out_ref[1] = jnp.where(is_zero, second, first).astype(out_ref.dtype)


def mix(pooled, partner_pool, self_pool, cross_pool, target, core, block):
    slots, flat = pooled.shape
    count = flat // (4 * block)
    shape = jax.ShapeDtypeStruct((2, slots, 2 * block), BF16)
    if (4 * block) % 128:
        width = self_pool.shape[0]
        mixed = (
            jnp.tile(self_pool, flat // width) * pooled.astype(F32)
            + jnp.tile(cross_pool, flat // width) * partner_pool.astype(F32)
        ).astype(BF16)
        mixed = mixed.reshape(slots, count, 2, 2, block).transpose(1, 2, 0, 3, 4).reshape(count, 2, slots, 2 * block)
        mixed = jnp.where(core == 0, mixed, mixed[:, ::-1])
        return [pick(mixed, target[p]) for p in range(count)]
    repeat = 4 * block // self_pool.shape[0]
    smem = pl.BlockSpec(memory_space=pltpu.SMEM)
    vmem = pl.BlockSpec(memory_space=pltpu.VMEM)
    return pl.pallas_call(
        functools.partial(mix_kernel, block),
        in_specs=[smem, smem, vmem, vmem, vmem, vmem],
        out_specs=[vmem] * count,
        out_shape=[shape] * count,
        compiler_params=pltpu.CompilerParams(vmem_limit_bytes=VMEM_LIMIT),
        cost_estimate=pl.CostEstimate(flops=0, bytes_accessed=0, transcendentals=0),
        name="mix",
    )(target, core[None], pooled, partner_pool, jnp.tile(self_pool, repeat)[None], jnp.tile(cross_pool, repeat)[None])


def join_kernel(block, count, width, target_ref, core_ref, cross_ref, pooled_ref, partner_ref, far_ref, *refs):
    here_refs = refs[:count]
    grad_ref, sent_ref, sums_ref = refs[count:]
    reach = 4 * block
    is_zero = core_ref[0] == 0
    own_sum = jnp.zeros((1, reach), F32)
    cross_sum = jnp.zeros((1, reach), F32)
    for p in range(count):
        lanes = pl.ds(pl.multiple_of(target_ref[p] * reach, 128), reach)
        here, there = here_refs[p][0].astype(F32), far_ref[p].astype(F32)
        zero, one = jnp.where(is_zero, here, there), jnp.where(is_zero, there, here)
        grad = jnp.concatenate([zero, one], axis=1)
        grad_ref[:, lanes] = grad.astype(grad_ref.dtype)
        sent_ref[:, lanes] = (cross_ref[...] * grad).astype(sent_ref.dtype)
        own_sum = own_sum + jnp.sum(pooled_ref[:, lanes].astype(F32) * grad, axis=0, keepdims=True)
        cross_sum = cross_sum + jnp.sum(partner_ref[:, lanes].astype(F32) * grad, axis=0, keepdims=True)
    for row, total in enumerate((own_sum, cross_sum)):
        folded = total[:, :width]
        for cell in range(1, reach // width):
            folded = folded + total[:, cell * width : (cell + 1) * width]
        sums_ref[row : row + 1, :] = folded


def join(here, far, pooled, partner_pool, cross_pool, target, core, block):
    slots, flat = pooled.shape
    count = flat // (4 * block)
    width = cross_pool.shape[0]
    if (4 * block) % 128:
        pieces = jnp.stack([jnp.stack([here[p][0], far[p]]) for p in range(count)])
        pieces = jnp.where(core == 0, pieces, pieces[:, ::-1]).reshape(count, 2, slots, 2, block)
        inverse = jnp.argsort(target)
        grad = jnp.take(pieces, inverse, axis=0).transpose(2, 0, 1, 3, 4).reshape(slots, flat)
        wide = grad.astype(F32)
        sent = (jnp.tile(cross_pool, flat // width) * wide).astype(BF16)
        sums = [
            jnp.sum(jnp.sum(a.astype(F32) * wide, axis=0).reshape(-1, width), axis=0) for a in (pooled, partner_pool)
        ]
        return grad, sent, jnp.stack(sums)
    smem = pl.BlockSpec(memory_space=pltpu.SMEM)
    vmem = pl.BlockSpec(memory_space=pltpu.VMEM)
    return pl.pallas_call(
        functools.partial(join_kernel, block, count, width),
        in_specs=[smem, smem] + [vmem] * (4 + count),
        out_specs=[vmem] * 3,
        out_shape=[
            jax.ShapeDtypeStruct((slots, flat), BF16),
            jax.ShapeDtypeStruct((slots, flat), BF16),
            jax.ShapeDtypeStruct((2, width), F32),
        ],
        compiler_params=pltpu.CompilerParams(vmem_limit_bytes=VMEM_LIMIT),
        cost_estimate=pl.CostEstimate(flops=0, bytes_accessed=0, transcendentals=0),
        name="join",
    )(target, core[None], jnp.tile(cross_pool, 4 * block // width)[None], pooled, partner_pool, far, *here)


def fc_forward_kernel(count, w_ref, got_ref, *refs):
    row_refs = refs[:count]
    chip_ref, sent_ref, all_ref = refs[count:]
    slots = got_ref.shape[1]

    @pl.when(pl.program_id(0) == 0)
    def _():
        for p in range(count):
            all_ref[pl.ds(p * slots, slots), :] = row_refs[p][0]
            all_ref[pl.ds((count + p) * slots, slots), :] = got_ref[p]

    total = jnp.dot(all_ref[...], w_ref[...], preferred_element_type=F32)
    half = count * slots
    for p in range(count):
        chip_ref[p] = total[p * slots : (p + 1) * slots]
        sent_ref[p] = total[half + p * slots : half + (p + 1) * slots].astype(sent_ref.dtype)


def fc_forward(rows, got, weight):
    count, (slots, depth), units = len(rows), got.shape[1:], weight.shape[1]
    tile = 1024
    if count > 4:
        used = jnp.concatenate([r[0] for r in rows] + [got.reshape(-1, depth)])
        total = jnp.dot(used, weight, preferred_element_type=F32).reshape(2, count, slots, units)
        return total[0], total[1].astype(BF16), used
    mine = pl.BlockSpec((1, slots, depth), lambda t: (0, 0, 0))
    out = pl.BlockSpec((count, slots, tile), lambda t: (0, 0, t))
    size = 2 * count * slots
    return pl.pallas_call(
        functools.partial(fc_forward_kernel, count),
        grid=(units // tile,),
        in_specs=[
            pl.BlockSpec((depth, tile), lambda t: (0, t)),
            pl.BlockSpec((count, slots, depth), lambda t: (0, 0, 0)),
        ]
        + [mine] * count,
        out_specs=[out, out, pl.BlockSpec((size, depth), lambda t: (0, 0))],
        out_shape=[
            jax.ShapeDtypeStruct((count, slots, units), F32),
            jax.ShapeDtypeStruct((count, slots, units), BF16),
            jax.ShapeDtypeStruct((size, depth), BF16),
        ],
        compiler_params=pltpu.CompilerParams(vmem_limit_bytes=VMEM_LIMIT),
        cost_estimate=pl.CostEstimate(flops=0, bytes_accessed=0, transcendentals=0),
        name="fc_forward",
    )(weight, got, *rows)


def fc_back_kernel(count, w_ref, own_ref, came_ref, *refs):
    out_refs, grads_ref = refs[:count], refs[count]
    slots, units = own_ref.shape[1:]
    half = count * slots

    @pl.when(pl.program_id(0) == 0)
    def _():
        grads_ref[:half] = own_ref[...].reshape(half, units)
        grads_ref[half:] = came_ref[...].reshape(half, units)

    total = lax.dot_general(grads_ref[...], w_ref[...], (((1,), (1,)), ((), ())), preferred_element_type=F32)
    for p, out_ref in enumerate(out_refs):
        for side in range(2):
            first = side * half + p * slots
            out_ref[side] = total[first : first + slots].astype(out_ref.dtype)


def fc_backward(own, came, weight):
    count, slots, units = own.shape
    depth = weight.shape[0]
    tile = 384 if depth % 384 == 0 else depth
    if count > 4:
        grads = jnp.stack([own, came], axis=1).reshape(-1, units)
        columns = lax.dot_general(grads, weight, (((1,), (1,)), ((), ())), preferred_element_type=F32)
        columns = columns.astype(BF16).reshape(count, 2, slots, depth)
        return [columns[p] for p in range(count)]
    grads = pl.BlockSpec((count, slots, units), lambda t: (0, 0, 0))
    return pl.pallas_call(
        functools.partial(fc_back_kernel, count),
        grid=(depth // tile,),
        in_specs=[pl.BlockSpec((tile, units), lambda t: (t, 0)), grads, grads],
        out_specs=[pl.BlockSpec((2, slots, tile), lambda t: (0, 0, t))] * count,
        out_shape=[jax.ShapeDtypeStruct((2, slots, depth), BF16)] * count,
        scratch_shapes=[pltpu.VMEM((2 * count * slots, units), BF16)],
        compiler_params=pltpu.CompilerParams(vmem_limit_bytes=VMEM_LIMIT),
        cost_estimate=pl.CostEstimate(flops=0, bytes_accessed=0, transcendentals=0),
        name="fc_backward",
    )(weight, own, came)


def halve_kernel(kept_ref, came_ref, out_ref, sent_ref):
    total = kept_ref[...] + came_ref[...].astype(F32)
    half = out_ref.shape[0]
    out_ref[...] = total[:half]
    sent_ref[...] = total[half:].astype(sent_ref.dtype)


def halve(kept, came):
    count, slots, units = kept.shape
    half = count // 2
    if count > 4:
        total = kept + came.astype(F32)
        return total[:half], total[half:].astype(BF16)
    tile = units // 4
    return pl.pallas_call(
        halve_kernel,
        grid=(4,),
        in_specs=[pl.BlockSpec((count, slots, tile), lambda t: (0, 0, t))] * 2,
        out_specs=[pl.BlockSpec((half, slots, tile), lambda t: (0, 0, t))] * 2,
        out_shape=[
            jax.ShapeDtypeStruct((half, slots, units), F32),
            jax.ShapeDtypeStruct((half, slots, units), BF16),
        ],
        compiler_params=pltpu.CompilerParams(vmem_limit_bytes=VMEM_LIMIT),
        cost_estimate=pl.CostEstimate(flops=0, bytes_accessed=0, transcendentals=0),
        name="halve",
    )(kept, came)


def hidden_kernel(kept_ref, came_ref, bias_ref, self_ref, cot_ref, scale_ref, back_ref, hidden_ref, grad_ref, sum_ref):
    pre = kept_ref[0] + came_ref[0].astype(F32) + bias_ref[...]
    hidden, slope = gelu_parts(pre)
    hidden_ref[...] = hidden.astype(hidden_ref.dtype)
    grad_out = cot_ref[...].astype(F32) * scale_ref[...]
    grad = ((self_ref[...] * grad_out + back_ref[...].astype(F32)) * slope).astype(grad_ref.dtype)
    grad_ref[0] = grad
    sum_ref[...] = jnp.sum(grad.astype(F32), axis=0, keepdims=True)


def hidden_step(n, kept, came, bias, self_fc, cotangent, scaling, back_fc):
    _, slots, units = kept.shape
    tile = units // 4
    one = pl.BlockSpec((1, tile), lambda t: (0, t))
    block = pl.BlockSpec((1, slots, tile), lambda t: (0, 0, t))
    rows = pl.BlockSpec((slots, tile), lambda t: (n, t))
    return pl.pallas_call(
        hidden_kernel,
        grid=(4,),
        in_specs=[block, block, one, one, rows, pl.BlockSpec((slots, 1), lambda t: (n, 0)), rows],
        out_specs=[pl.BlockSpec((slots, tile), lambda t: (0, t)), block, one],
        out_shape=[
            jax.ShapeDtypeStruct((slots, units), BF16),
            jax.ShapeDtypeStruct((1, slots, units), BF16),
            jax.ShapeDtypeStruct((1, units), F32),
        ],
        compiler_params=pltpu.CompilerParams(vmem_limit_bytes=VMEM_LIMIT),
        cost_estimate=pl.CostEstimate(flops=0, bytes_accessed=0, transcendentals=0),
        name="hidden",
    )(kept, came, bias[None], self_fc[None], cotangent, scaling[:, None], back_fc)


def unwritten(shape, dtype):
    return pl.pallas_call(
        lambda ref: None,
        out_specs=pl.BlockSpec(memory_space=pl.ANY),
        out_shape=jax.ShapeDtypeStruct(shape, dtype),
        cost_estimate=pl.CostEstimate(flops=0, bytes_accessed=0, transcendentals=0),
        name="unwritten",
    )()


def gelu_parts(v):
    root = 0.7978845608028654
    cubic = 0.044715
    square = v * v
    half = 0.5 + 0.5 * jnp.tanh(v * (root + (root * cubic) * square))
    slope = half + (half * (1.0 - half)) * (v * (2.0 * root + (6.0 * root * cubic) * square))
    return v * half, slope


def conv_forward(inputs, kernel, bias):
    pre_conv = lax.conv_general_dilated(
        inputs, kernel, (1, 1), ((1, 1), (1, 1)), dimension_numbers=CONV_DIMS, preferred_element_type=F32
    )
    activity, slope = gelu_parts(pre_conv + bias)
    e = jnp.exp(activity)
    return e.astype(BF16), ((0.5 * e) * slope).astype(BF16)


def conv_grad_inputs(grad_pre, kernel):
    turned = jnp.flip(kernel, (0, 1)).swapaxes(2, 3)
    return lax.conv_general_dilated(
        grad_pre, turned, (1, 1), ((1, 1), (1, 1)), dimension_numbers=CONV_DIMS, preferred_element_type=F32
    ).astype(BF16)


def conv_grad_kernel(inputs, grad_pre):
    dims = lax.ConvDimensionNumbers(lhs_spec=(3, 0, 1, 2), rhs_spec=(3, 0, 1, 2), out_spec=(2, 3, 0, 1))
    return lax.conv_general_dilated(
        inputs, grad_pre, (1, 1), ((1, 1), (1, 1)), dimension_numbers=dims, preferred_element_type=F32
    )


def sum_small(vector):
    vector = vector + swap_core(vector)
    vector = vector + swap_mid(vector)
    step = 1
    while step < lax.axis_size("outer"):
        vector = vector + swap_outer(vector, step)
        step *= 2
    return vector


def sum_kernel(rows, outer, mid, core):
    outer_count = lax.axis_size("outer")
    for swap, side in ((swap_mid, mid), (swap_core, core)):
        halves = rows.reshape(2, -1, rows.shape[1])
        got = swap(pick(halves, 1 - side).astype(BF16))
        rows = pick(halves, side) + got.astype(F32)
    parts = rows.reshape(outer_count, -1, rows.shape[1])
    total = pick(parts, outer)
    for k in range(1, outer_count):
        total = total + swap_outer(pick(parts, outer ^ k).astype(BF16), k).astype(F32)
    total = total.astype(BF16)
    stack = jnp.stack([total] + [swap_outer(total, k) for k in range(1, outer_count)])
    rows = jnp.concatenate([pick(stack, outer ^ k) for k in range(outer_count)])
    for swap, side in ((swap_core, core), (swap_mid, mid)):
        got = swap(rows)
        rows = jnp.where(side == 0, jnp.concatenate([rows, got]), jnp.concatenate([got, rows]))
    return rows.astype(F32)


def body(
    features,
    conv_weight,
    conv_bias,
    fc_weight,
    fc_bias,
    stitch_pool,
    stitch_fc,
    cotangent,
    crop_counts,
    slot_image,
    slot_mask,
):
    is_first = lax.axis_index("tower") == 0
    core, mid, outer = lax.axis_index("core"), lax.axis_index("mid"), lax.axis_index("outer")
    outer_count = lax.axis_size("outer")
    block, units = fc_weight.shape[1:]
    weight = lax.all_gather(fc_weight[0], "mid", axis=0, tiled=True)

    row_pool = stitch_pool[0]
    self_pool = jnp.where(is_first, row_pool[0], row_pool[1])
    cross_pool = jnp.where(is_first, row_pool[1], row_pool[0])
    row_fc = stitch_fc[0]
    self_fc = jnp.where(is_first, row_fc[0], row_fc[1])
    cross_fc = jnp.where(is_first, row_fc[1], row_fc[0])

    live_slots = slot_mask.astype(F32)
    image_ids = jnp.arange(crop_counts.shape[0], dtype=jnp.int32)
    matches = (slot_image[:, None] == image_ids[None, :]).astype(F32)
    per_slot = jnp.sum(matches * crop_counts.astype(F32)[None, :], axis=1)
    scaling = live_slots / per_slot
    sent_fc = (cross_fc * (cotangent[0].astype(F32) * scaling[:, None])).astype(BF16)
    back_fc = swap_tower(sent_fc)

    inputs = features[0]
    kernel = conv_weight[0]
    width = kernel.shape[3]
    hops = outer_count.bit_length() - 1
    order = [sum(((p >> b) & 1) << (hops - 1 - b) for b in range(hops)) for p in range(outer_count)]
    target = outer ^ jnp.array(order, jnp.int32)
    total_slots = inputs.shape[0]
    sizes = [total_slots // 4] * 4 if outer_count <= 4 else [total_slots]
    starts = [sum(sizes[:n]) for n in range(len(sizes))]
    last = [scaling]

    def after(array):
        return lax.optimization_barrier((array, last[0]))[0]

    sums = dict(fc_bias=0.0, pool=0.0, conv_bias=0.0, kernel=0.0)
    stage = {}
    hiddens = {}
    count, extent, _, depth = inputs.shape
    stage["grad_in"] = jnp.transpose(unwritten((extent, extent, count, depth), BF16), (2, 0, 1, 3))
    lead = (((0,), (0,)), ((), ()))

    def chunk(n):
        slots = sizes[n]
        rows = slice(starts[n], starts[n] + slots)
        part = inputs[rows]
        e, slope = conv_forward(part, kernel, after(conv_bias[0]))
        pooled, inv = pool_forward(jnp.transpose(e, (1, 2, 0, 3)))
        last[0] = pooled
        partner_pool = swap_tower(pooled)
        yield
        rows_of = mix(after(pooled), partner_pool, self_pool, cross_pool, target, core, block)
        last[0] = rows_of[0]
        arrived = [rows_of[0]] + [swap_outer(r, k) for r, k in zip(rows_of[1:], order[1:])]
        yield
        arrived[0] = after(arrived[0])
        give = jnp.stack([r[1] for r in arrived])
        last[0] = give
        got = swap_core(give)
        yield
        chip, sent, flat = fc_forward(arrived, after(got), weight)
        last[0] = sent
        came = swap_core(sent)
        yield
        for hop in range(hops):
            chip, sent = halve(chip, after(came))
            last[0] = sent
            came = swap_outer(sent, 1 << hop)
            yield
        hiddens[n], gathered, bias_sum = hidden_step(
            n, chip, after(came), fc_bias[0], self_fc, cotangent[0], scaling, back_fc
        )
        sums["fc_bias"] += bias_sum[0]
        last[0] = gathered
        for hop in reversed(range(hops)):
            came = swap_outer(gathered, 1 << hop)
            yield
            gathered = jnp.concatenate([gathered, after(came)])
            last[0] = gathered
        came = swap_core(gathered)
        yield
        came = after(came)
        stage[n] = (flat, gathered, came)
        columns = fc_backward(gathered, came, weight)
        last[0] = columns[0]
        arrived = [columns[0]] + [swap_outer(c, k) for c, k in zip(columns[1:], order[1:])]
        yield
        arrived[0] = after(arrived[0])
        give = jnp.stack([r[1] for r in arrived])
        last[0] = give
        far = swap_core(give)
        yield
        grad_mixed, sent, stitch_sums = join(
            arrived, after(far), pooled, partner_pool, cross_pool, target, core, block
        )
        sums["pool"] += stitch_sums
        last[0] = sent
        back_pool = swap_tower(sent)
        yield
        grad_pre, bias_rows = pool_backward(
            jnp.transpose(slope, (1, 2, 0, 3)), grad_mixed, after(back_pool), inv, self_pool
        )
        sums["conv_bias"] += jnp.sum(bias_rows, axis=0)
        grad_pre = jnp.transpose(grad_pre, (2, 0, 1, 3))
        grad_kernel = conv_grad_kernel(part, grad_pre)
        sums["kernel"] += grad_kernel
        last[0] = grad_kernel
        yield
        part = conv_grad_inputs(after(grad_pre), kernel)
        stage["grad_in"] = lax.dynamic_update_slice(stage["grad_in"], part, (starts[n], 0, 0, 0))
        last[0] = stage["grad_in"]

    def stitch():
        hidden = after(jnp.concatenate([hiddens[n] for n in range(len(sizes))]))
        last[0] = hidden
        partner_hidden = swap_tower(hidden)
        yield
        partner_hidden = after(partner_hidden).astype(F32)
        hidden = hidden.astype(F32)
        stage["output"] = ((self_fc * hidden + cross_fc * partner_hidden) * live_slots[:, None]).astype(BF16)
        grad_out = cotangent[0].astype(F32) * scaling[:, None]
        stage["hidden"] = jnp.sum(hidden * grad_out, axis=0), jnp.sum(partner_hidden * grad_out, axis=0)
        last[0] = stage["output"]

    def fc_weight_gradient():
        columns = jnp.concatenate([stage[n][0] for n in range(len(sizes))])
        grads = after(jnp.concatenate([g.reshape(-1, units) for n in range(len(sizes)) for g in stage[n][1:]]))
        own, far = columns[:, :block], columns[:, block:]
        own, far = jnp.where(mid == 0, own, far), jnp.where(mid == 0, far, own)
        far_term = lax.dot_general(far, grads, lead, preferred_element_type=F32).astype(BF16)
        last[0] = far_term
        came = swap_mid(far_term)
        yield
        own, came = lax.optimization_barrier((own, after(came)))
        stage["gradient"] = lax.dot_general(own, grads, lead, preferred_element_type=F32) + came.astype(F32)
        last[0] = stage["gradient"]

    runs = {str(n): chunk(n) for n in range(len(sizes))}
    runs.update(W=fc_weight_gradient(), S=stitch())
    for n in PLAN if len(sizes) > 1 else "0" * (2 * hops + 6) + "WS" + "0" * 5 + "WS":
        next(runs[n], None)
    grad_fc_weight = stage["gradient"]
    kernel_sum = sums["kernel"]
    conv_bias_sum, fc_bias_sum = sums["conv_bias"], sums["fc_bias"]
    hidden_self, hidden_cross = stage["hidden"]
    pool_self, pool_cross = sums["pool"]

    small = sum_small(
        jnp.concatenate([conv_bias_sum, pool_self, pool_cross, fc_bias_sum, hidden_self, hidden_cross])[None]
    )[0]
    cuts = [width, 2 * width, 3 * width, 3 * width + units, 3 * width + 2 * units]
    conv_bias_sum, pool_self, pool_cross, fc_bias_sum, hidden_self, hidden_cross = jnp.split(small, cuts)
    grad_row_pool = jnp.where(
        is_first, jnp.stack([pool_self, pool_cross]), jnp.stack([pool_cross, pool_self])
    )
    grad_row_fc = jnp.where(
        is_first, jnp.stack([hidden_self, hidden_cross]), jnp.stack([hidden_cross, hidden_self])
    )
    summed_kernel = sum_kernel(kernel_sum.reshape(-1, width), outer, mid, core).reshape(kernel.shape)
    return (
        stage["output"][None],
        stage["grad_in"][None],
        summed_kernel[None],
        conv_bias_sum[None],
        grad_fc_weight[None],
        fc_bias_sum[None],
        grad_row_pool[None],
        grad_row_fc[None],
    )


def solution(mesh):
    mesh = jax.sharding.Mesh(mesh.devices.reshape(mesh.shape["tower"], -1, 2, 2), ("tower", "outer", "core", "mid"))
    crops = ("outer", "core", "mid")
    placed = (
        P("tower", crops, None, None, None),
        P("tower", None, None, None, None),
        P("tower", None),
        P("tower", crops, None),
        P("tower", None),
        P("tower", None, None),
        P("tower", None, None),
        P("tower", crops, None),
        P(crops),
        P(crops),
        P(crops),
    )
    return jax.shard_map(
        body,
        mesh=mesh,
        in_specs=placed,
        out_specs=(
            P("tower", crops, None),
            P("tower", crops, None, None, None),
            P("tower", None, None, None, None),
            P("tower", None),
            P("tower", crops, None),
            P("tower", None),
            P("tower", None, None),
            P("tower", None, None),
        ),
        check_vma=False,
    )
```

```python
import functools

import jax
import jax.numpy as jnp
from jax import lax
from jax.experimental import pallas as pl
from jax.experimental.pallas import tpu as pltpu
from jax.sharding import PartitionSpec as P

PLAN = "0102010213012301320130210321301230210231S021302123W23W3S3AA1A2A3AAA"
BF16 = jnp.bfloat16
F32 = jnp.float32
CONV_DIMS = ("NHWC", "HWIO", "NHWC")
VMEM_LIMIT = 48 * 1024 * 1024


def swap_core(block):
    return lax.ppermute(block, "core", [(0, 1), (1, 0)])


def swap_mid(block):
    return lax.ppermute(block, "mid", [(0, 1), (1, 0)])


def swap_outer(block, mask):
    count = lax.axis_size("outer")
    return lax.ppermute(block, "outer", [(i, i ^ mask) for i in range(count)])


def swap_tower(block):
    return lax.ppermute(block, "tower", [(0, 1), (1, 0)])


def pick(stack, index):
    return lax.dynamic_index_in_dim(stack, index, 0, keepdims=False)


def pool_kernel(e_ref, pooled_ref, inv_ref):
    extent = e_ref.shape[0]
    width = e_ref.shape[3]
    out = (extent - 3) // 2 + 1

    def columns(row):
        cells = [e_ref[row, col].astype(F32) for col in range(extent)]
        return [cells[2 * j] + cells[2 * j + 1] + cells[2 * j + 2] for j in range(out)]

    top = columns(0)
    for i in range(out):
        middle = columns(2 * i + 1)
        bottom = columns(2 * i + 2)
        for j in range(out):
            total = top[j] + middle[j] + bottom[j]
            lanes = pl.ds((i * out + j) * width, width)
            pooled_ref[:, lanes] = jnp.log(total).astype(pooled_ref.dtype)
            inv_ref[:, lanes] = 2.0 / total
        top = bottom


def pool_forward(e):
    extent, _, slots, width = e.shape
    out = (extent - 3) // 2 + 1
    block = 16
    flat = out * out * width
    return pl.pallas_call(
        pool_kernel,
        grid=(slots // block,),
        in_specs=[pl.BlockSpec((extent, extent, block, width), lambda s: (0, 0, s, 0))],
        out_specs=[
            pl.BlockSpec((block, flat), lambda s: (s, 0)),
            pl.BlockSpec((block, flat), lambda s: (s, 0)),
        ],
        out_shape=[
            jax.ShapeDtypeStruct((slots, flat), BF16),
            jax.ShapeDtypeStruct((slots, flat), F32),
        ],
        compiler_params=pltpu.CompilerParams(vmem_limit_bytes=VMEM_LIMIT),
        cost_estimate=pl.CostEstimate(flops=0, bytes_accessed=0, transcendentals=0),
        name="pool_forward",
    )(e)


def pool_back_kernel(slope_ref, grad_ref, back_ref, inv_ref, self_ref, g_ref, bias_ref):
    extent = slope_ref.shape[0]
    width = slope_ref.shape[3]
    out = (extent - 3) // 2 + 1
    coef = self_ref[0:1, :]

    @pl.when(pl.program_id(0) == 0)
    def _():
        bias_ref[...] = jnp.zeros_like(bias_ref)

    def window_row(i):
        row = []
        for j in range(out):
            lanes = pl.ds((i * out + j) * width, width)
            grad = coef * grad_ref[:, lanes].astype(F32) + back_ref[:, lanes].astype(F32)
            row.append(grad * inv_ref[:, lanes])
        return row

    sums = jnp.zeros((slope_ref.shape[2], width), F32)
    above = None
    current = window_row(0)
    for row in range(extent):
        if row % 2 == 0:
            if row == 0:
                rows = current
            elif row == extent - 1:
                rows = current
            else:
                above, current = current, window_row(row // 2)
                rows = [a + b for a, b in zip(above, current)]
        else:
            rows = current
        for col in range(extent):
            if col % 2 == 1:
                spread = rows[col // 2]
            elif col == 0:
                spread = rows[0]
            elif col == extent - 1:
                spread = rows[out - 1]
            else:
                spread = rows[col // 2 - 1] + rows[col // 2]
            grad = (slope_ref[row, col].astype(F32) * spread).astype(g_ref.dtype)
            g_ref[row, col] = grad
            sums = sums + grad.astype(F32)
    bias_ref[...] += sums


def pool_backward(slope, grad_mixed, back_pool, inv, self_pool):
    extent, _, slots, width = slope.shape
    block = 16
    flat = grad_mixed.shape[1]
    rows = pl.BlockSpec((block, flat), lambda s: (s, 0))
    grid_block = pl.BlockSpec((extent, extent, block, width), lambda s: (0, 0, s, 0))
    return pl.pallas_call(
        pool_back_kernel,
        grid=(slots // block,),
        in_specs=[grid_block, rows, rows, rows, pl.BlockSpec((1, width), lambda s: (0, 0))],
        out_specs=[grid_block, pl.BlockSpec((block, width), lambda s: (0, 0))],
        out_shape=[
            jax.ShapeDtypeStruct(slope.shape, BF16),
            jax.ShapeDtypeStruct((block, width), F32),
        ],
        compiler_params=pltpu.CompilerParams(vmem_limit_bytes=VMEM_LIMIT),
        cost_estimate=pl.CostEstimate(flops=0, bytes_accessed=0, transcendentals=0),
        name="pool_backward",
    )(slope, grad_mixed, back_pool, inv, self_pool[None])


def mix_kernel(block, target_ref, core_ref, pooled_ref, partner_ref, self_ref, cross_ref, *out_refs):
    reach = 4 * block
    is_zero = core_ref[0] == 0
    for p, out_ref in enumerate(out_refs):
        lanes = pl.ds(pl.multiple_of(target_ref[p] * reach, 128), reach)
        mixed = self_ref[...] * pooled_ref[:, lanes].astype(F32) + cross_ref[...] * partner_ref[:, lanes].astype(F32)
        first = mixed[:, : 2 * block]
        second = mixed[:, 2 * block :]
        out_ref[0] = jnp.where(is_zero, first, second).astype(out_ref.dtype)
        out_ref[1] = jnp.where(is_zero, second, first).astype(out_ref.dtype)


def mix(pooled, partner_pool, self_pool, cross_pool, target, core, block):
    slots, flat = pooled.shape
    count = flat // (4 * block)
    shape = jax.ShapeDtypeStruct((2, slots, 2 * block), BF16)
    if (4 * block) % 128:
        width = self_pool.shape[0]
        mixed = (
            jnp.tile(self_pool, flat // width) * pooled.astype(F32)
            + jnp.tile(cross_pool, flat // width) * partner_pool.astype(F32)
        ).astype(BF16)
        mixed = mixed.reshape(slots, count, 2, 2, block).transpose(1, 2, 0, 3, 4).reshape(count, 2, slots, 2 * block)
        mixed = jnp.where(core == 0, mixed, mixed[:, ::-1])
        return [pick(mixed, target[p]) for p in range(count)]
    repeat = 4 * block // self_pool.shape[0]
    smem = pl.BlockSpec(memory_space=pltpu.SMEM)
    vmem = pl.BlockSpec(memory_space=pltpu.VMEM)
    return pl.pallas_call(
        functools.partial(mix_kernel, block),
        in_specs=[smem, smem, vmem, vmem, vmem, vmem],
        out_specs=[vmem] * count,
        out_shape=[shape] * count,
        compiler_params=pltpu.CompilerParams(vmem_limit_bytes=VMEM_LIMIT),
        cost_estimate=pl.CostEstimate(flops=0, bytes_accessed=0, transcendentals=0),
        name="mix",
    )(target, core[None], pooled, partner_pool, jnp.tile(self_pool, repeat)[None], jnp.tile(cross_pool, repeat)[None])


def join_kernel(block, count, width, target_ref, core_ref, cross_ref, pooled_ref, partner_ref, far_ref, *refs):
    here_refs = refs[:count]
    grad_ref, sent_ref, sums_ref = refs[count:]
    reach = 4 * block
    is_zero = core_ref[0] == 0
    own_sum = jnp.zeros((1, reach), F32)
    cross_sum = jnp.zeros((1, reach), F32)
    for p in range(count):
        lanes = pl.ds(pl.multiple_of(target_ref[p] * reach, 128), reach)
        here, there = here_refs[p][0].astype(F32), far_ref[p].astype(F32)
        zero, one = jnp.where(is_zero, here, there), jnp.where(is_zero, there, here)
        grad = jnp.concatenate([zero, one], axis=1)
        grad_ref[:, lanes] = grad.astype(grad_ref.dtype)
        sent_ref[:, lanes] = (cross_ref[...] * grad).astype(sent_ref.dtype)
        own_sum = own_sum + jnp.sum(pooled_ref[:, lanes].astype(F32) * grad, axis=0, keepdims=True)
        cross_sum = cross_sum + jnp.sum(partner_ref[:, lanes].astype(F32) * grad, axis=0, keepdims=True)
    for row, total in enumerate((own_sum, cross_sum)):
        folded = total[:, :width]
        for cell in range(1, reach // width):
            folded = folded + total[:, cell * width : (cell + 1) * width]
        sums_ref[row : row + 1, :] = folded


def join(here, far, pooled, partner_pool, cross_pool, target, core, block):
    slots, flat = pooled.shape
    count = flat // (4 * block)
    width = cross_pool.shape[0]
    if (4 * block) % 128:
        pieces = jnp.stack([jnp.stack([here[p][0], far[p]]) for p in range(count)])
        pieces = jnp.where(core == 0, pieces, pieces[:, ::-1]).reshape(count, 2, slots, 2, block)
        inverse = jnp.argsort(target)
        grad = jnp.take(pieces, inverse, axis=0).transpose(2, 0, 1, 3, 4).reshape(slots, flat)
        wide = grad.astype(F32)
        sent = (jnp.tile(cross_pool, flat // width) * wide).astype(BF16)
        sums = [
            jnp.sum(jnp.sum(a.astype(F32) * wide, axis=0).reshape(-1, width), axis=0) for a in (pooled, partner_pool)
        ]
        return grad, sent, jnp.stack(sums)
    smem = pl.BlockSpec(memory_space=pltpu.SMEM)
    vmem = pl.BlockSpec(memory_space=pltpu.VMEM)
    return pl.pallas_call(
        functools.partial(join_kernel, block, count, width),
        in_specs=[smem, smem] + [vmem] * (4 + count),
        out_specs=[vmem] * 3,
        out_shape=[
            jax.ShapeDtypeStruct((slots, flat), BF16),
            jax.ShapeDtypeStruct((slots, flat), BF16),
            jax.ShapeDtypeStruct((2, width), F32),
        ],
        compiler_params=pltpu.CompilerParams(vmem_limit_bytes=VMEM_LIMIT),
        cost_estimate=pl.CostEstimate(flops=0, bytes_accessed=0, transcendentals=0),
        name="join",
    )(target, core[None], jnp.tile(cross_pool, 4 * block // width)[None], pooled, partner_pool, far, *here)


def fc_forward_kernel(count, w_ref, got_ref, *refs):
    row_refs = refs[:count]
    chip_ref, sent_ref, all_ref = refs[count:]
    slots = got_ref.shape[1]

    @pl.when(pl.program_id(0) == 0)
    def _():
        for p in range(count):
            all_ref[pl.ds(p * slots, slots), :] = row_refs[p][0]
            all_ref[pl.ds((count + p) * slots, slots), :] = got_ref[p]

    total = jnp.dot(all_ref[...], w_ref[...], preferred_element_type=F32)
    half = count * slots
    for p in range(count):
        chip_ref[p] = total[p * slots : (p + 1) * slots]
        sent_ref[p] = total[half + p * slots : half + (p + 1) * slots].astype(sent_ref.dtype)


def fc_forward(rows, got, weight):
    count, (slots, depth), units = len(rows), got.shape[1:], weight.shape[1]
    tile = 1024
    if count > 4:
        used = jnp.concatenate([r[0] for r in rows] + [got.reshape(-1, depth)])
        total = jnp.dot(used, weight, preferred_element_type=F32).reshape(2, count, slots, units)
        return total[0], total[1].astype(BF16), used
    mine = pl.BlockSpec((1, slots, depth), lambda t: (0, 0, 0))
    out = pl.BlockSpec((count, slots, tile), lambda t: (0, 0, t))
    size = 2 * count * slots
    return pl.pallas_call(
        functools.partial(fc_forward_kernel, count),
        grid=(units // tile,),
        in_specs=[
            pl.BlockSpec((depth, tile), lambda t: (0, t)),
            pl.BlockSpec((count, slots, depth), lambda t: (0, 0, 0)),
        ]
        + [mine] * count,
        out_specs=[out, out, pl.BlockSpec((size, depth), lambda t: (0, 0))],
        out_shape=[
            jax.ShapeDtypeStruct((count, slots, units), F32),
            jax.ShapeDtypeStruct((count, slots, units), BF16),
            jax.ShapeDtypeStruct((size, depth), BF16),
        ],
        compiler_params=pltpu.CompilerParams(vmem_limit_bytes=VMEM_LIMIT),
        cost_estimate=pl.CostEstimate(flops=0, bytes_accessed=0, transcendentals=0),
        name="fc_forward",
    )(weight, got, *rows)


def fc_back_kernel(count, w_ref, own_ref, came_ref, *refs):
    out_refs, grads_ref = refs[:count], refs[count]
    slots, units = own_ref.shape[1:]
    half = count * slots

    @pl.when(pl.program_id(0) == 0)
    def _():
        grads_ref[:half] = own_ref[...].reshape(half, units)
        grads_ref[half:] = came_ref[...].reshape(half, units)

    total = lax.dot_general(grads_ref[...], w_ref[...], (((1,), (1,)), ((), ())), preferred_element_type=F32)
    for p, out_ref in enumerate(out_refs):
        for side in range(2):
            first = side * half + p * slots
            out_ref[side] = total[first : first + slots].astype(out_ref.dtype)


def fc_backward(own, came, weight):
    count, slots, units = own.shape
    depth = weight.shape[0]
    tile = 384 if depth % 384 == 0 else depth
    if count > 4:
        grads = jnp.stack([own, came], axis=1).reshape(-1, units)
        columns = lax.dot_general(grads, weight, (((1,), (1,)), ((), ())), preferred_element_type=F32)
        columns = columns.astype(BF16).reshape(count, 2, slots, depth)
        return [columns[p] for p in range(count)]
    grads = pl.BlockSpec((count, slots, units), lambda t: (0, 0, 0))
    return pl.pallas_call(
        functools.partial(fc_back_kernel, count),
        grid=(depth // tile,),
        in_specs=[pl.BlockSpec((tile, units), lambda t: (t, 0)), grads, grads],
        out_specs=[pl.BlockSpec((2, slots, tile), lambda t: (0, 0, t))] * count,
        out_shape=[jax.ShapeDtypeStruct((2, slots, depth), BF16)] * count,
        scratch_shapes=[pltpu.VMEM((2 * count * slots, units), BF16)],
        compiler_params=pltpu.CompilerParams(vmem_limit_bytes=VMEM_LIMIT),
        cost_estimate=pl.CostEstimate(flops=0, bytes_accessed=0, transcendentals=0),
        name="fc_backward",
    )(weight, own, came)


def halve_kernel(kept_ref, came_ref, out_ref, sent_ref):
    total = kept_ref[...] + came_ref[...].astype(F32)
    half = out_ref.shape[0]
    out_ref[...] = total[:half]
    sent_ref[...] = total[half:].astype(sent_ref.dtype)


def halve(kept, came):
    count, slots, units = kept.shape
    half = count // 2
    if count > 4:
        total = kept + came.astype(F32)
        return total[:half], total[half:].astype(BF16)
    tile = units // 4
    return pl.pallas_call(
        halve_kernel,
        grid=(4,),
        in_specs=[pl.BlockSpec((count, slots, tile), lambda t: (0, 0, t))] * 2,
        out_specs=[pl.BlockSpec((half, slots, tile), lambda t: (0, 0, t))] * 2,
        out_shape=[
            jax.ShapeDtypeStruct((half, slots, units), F32),
            jax.ShapeDtypeStruct((half, slots, units), BF16),
        ],
        compiler_params=pltpu.CompilerParams(vmem_limit_bytes=VMEM_LIMIT),
        cost_estimate=pl.CostEstimate(flops=0, bytes_accessed=0, transcendentals=0),
        name="halve",
    )(kept, came)


def hidden_kernel(kept_ref, came_ref, bias_ref, self_ref, cot_ref, scale_ref, back_ref, hidden_ref, grad_ref, sum_ref):
    pre = kept_ref[0] + came_ref[0].astype(F32) + bias_ref[...]
    hidden, slope = gelu_parts(pre)
    hidden_ref[...] = hidden.astype(hidden_ref.dtype)
    grad_out = cot_ref[...].astype(F32) * scale_ref[...]
    grad = ((self_ref[...] * grad_out + back_ref[...].astype(F32)) * slope).astype(grad_ref.dtype)
    grad_ref[0] = grad
    sum_ref[...] = jnp.sum(grad.astype(F32), axis=0, keepdims=True)


def hidden_step(n, kept, came, bias, self_fc, cotangent, scaling, back_fc):
    _, slots, units = kept.shape
    tile = units // 4
    one = pl.BlockSpec((1, tile), lambda t: (0, t))
    block = pl.BlockSpec((1, slots, tile), lambda t: (0, 0, t))
    rows = pl.BlockSpec((slots, tile), lambda t: (n, t))
    return pl.pallas_call(
        hidden_kernel,
        grid=(4,),
        in_specs=[block, block, one, one, rows, pl.BlockSpec((slots, 1), lambda t: (n, 0)), rows],
        out_specs=[pl.BlockSpec((slots, tile), lambda t: (0, t)), block, one],
        out_shape=[
            jax.ShapeDtypeStruct((slots, units), BF16),
            jax.ShapeDtypeStruct((1, slots, units), BF16),
            jax.ShapeDtypeStruct((1, units), F32),
        ],
        compiler_params=pltpu.CompilerParams(vmem_limit_bytes=VMEM_LIMIT),
        cost_estimate=pl.CostEstimate(flops=0, bytes_accessed=0, transcendentals=0),
        name="hidden",
    )(kept, came, bias[None], self_fc[None], cotangent, scaling[:, None], back_fc)


def unwritten(shape, dtype):
    return pl.pallas_call(
        lambda ref: None,
        out_specs=pl.BlockSpec(memory_space=pl.ANY),
        out_shape=jax.ShapeDtypeStruct(shape, dtype),
        cost_estimate=pl.CostEstimate(flops=0, bytes_accessed=0, transcendentals=0),
        name="unwritten",
    )()


def gelu_parts(v):
    root = 0.7978845608028654
    cubic = 0.044715
    square = v * v
    half = 0.5 + 0.5 * jnp.tanh(v * (root + (root * cubic) * square))
    slope = half + (half * (1.0 - half)) * (v * (2.0 * root + (6.0 * root * cubic) * square))
    return v * half, slope


def conv_forward(inputs, kernel, bias):
    pre_conv = lax.conv_general_dilated(
        inputs, kernel, (1, 1), ((1, 1), (1, 1)), dimension_numbers=CONV_DIMS, preferred_element_type=F32
    )
    activity, slope = gelu_parts(pre_conv + bias)
    e = jnp.exp(activity)
    return e.astype(BF16), ((0.5 * e) * slope).astype(BF16)


def conv_grad_inputs(grad_pre, kernel):
    turned = jnp.flip(kernel, (0, 1)).swapaxes(2, 3)
    return lax.conv_general_dilated(
        grad_pre, turned, (1, 1), ((1, 1), (1, 1)), dimension_numbers=CONV_DIMS, preferred_element_type=F32
    ).astype(BF16)


def conv_grad_kernel(inputs, grad_pre):
    dims = lax.ConvDimensionNumbers(lhs_spec=(3, 0, 1, 2), rhs_spec=(3, 0, 1, 2), out_spec=(2, 3, 0, 1))
    return lax.conv_general_dilated(
        inputs, grad_pre, (1, 1), ((1, 1), (1, 1)), dimension_numbers=dims, preferred_element_type=F32
    )


def sum_small(vector):
    vector = vector + swap_core(vector)
    vector = vector + swap_mid(vector)
    step = 1
    while step < lax.axis_size("outer"):
        vector = vector + swap_outer(vector, step)
        step *= 2
    return vector


def sum_kernel(stage, last, after, rows, outer, mid, core):
    outer_count = lax.axis_size("outer")
    for swap, side in ((swap_mid, mid), (swap_core, core)):
        halves = rows.reshape(2, -1, rows.shape[1])
        sent, kept = pick(halves, 1 - side).astype(BF16), pick(halves, side)
        last[0] = sent
        got = swap(sent)
        yield
        rows = kept + after(got).astype(F32)
    parts = rows.reshape(outer_count, -1, rows.shape[1])
    total = pick(parts, outer)
    sent = [pick(parts, outer ^ k).astype(BF16) for k in range(1, outer_count)]
    last[0] = sent[-1]
    got = [swap_outer(s, k + 1) for k, s in enumerate(sent)]
    yield
    got[0] = after(got[0])
    for g in got:
        total = total + g.astype(F32)
    total = total.astype(BF16)
    last[0] = total
    stack = [total] + [swap_outer(total, k) for k in range(1, outer_count)]
    yield
    stack = jnp.stack([after(total), *stack[1:]])
    rows = jnp.concatenate([pick(stack, outer ^ k) for k in range(outer_count)])
    for swap, side in ((swap_core, core), (swap_mid, mid)):
        last[0] = rows
        got = swap(rows)
        yield
        got = after(got)
        rows = jnp.where(side == 0, jnp.concatenate([rows, got]), jnp.concatenate([got, rows]))
    stage["kernel"] = rows.astype(F32)


def body(
    features,
    conv_weight,
    conv_bias,
    fc_weight,
    fc_bias,
    stitch_pool,
    stitch_fc,
    cotangent,
    crop_counts,
    slot_image,
    slot_mask,
):
    is_first = lax.axis_index("tower") == 0
    core, mid, outer = lax.axis_index("core"), lax.axis_index("mid"), lax.axis_index("outer")
    outer_count = lax.axis_size("outer")
    block, units = fc_weight.shape[1:]
    weight = lax.all_gather(fc_weight[0], "mid", axis=0, tiled=True)

    row_pool = stitch_pool[0]
    self_pool = jnp.where(is_first, row_pool[0], row_pool[1])
    cross_pool = jnp.where(is_first, row_pool[1], row_pool[0])
    row_fc = stitch_fc[0]
    self_fc = jnp.where(is_first, row_fc[0], row_fc[1])
    cross_fc = jnp.where(is_first, row_fc[1], row_fc[0])

    live_slots = slot_mask.astype(F32)
    image_ids = jnp.arange(crop_counts.shape[0], dtype=jnp.int32)
    matches = (slot_image[:, None] == image_ids[None, :]).astype(F32)
    per_slot = jnp.sum(matches * crop_counts.astype(F32)[None, :], axis=1)
    scaling = live_slots / per_slot
    sent_fc = (cross_fc * (cotangent[0].astype(F32) * scaling[:, None])).astype(BF16)
    back_fc = swap_tower(sent_fc)

    inputs = features[0]
    kernel = conv_weight[0]
    width = kernel.shape[3]
    hops = outer_count.bit_length() - 1
    order = [sum(((p >> b) & 1) << (hops - 1 - b) for b in range(hops)) for p in range(outer_count)]
    target = outer ^ jnp.array(order, jnp.int32)
    total_slots = inputs.shape[0]
    sizes = [total_slots // 4] * 4 if outer_count <= 4 else [total_slots]
    starts = [sum(sizes[:n]) for n in range(len(sizes))]
    last = [scaling]

    def after(array):
        return lax.optimization_barrier((array, last[0]))[0]

    sums = dict(fc_bias=0.0, pool=0.0, conv_bias=0.0, kernel=0.0)
    stage = {}
    hiddens = {}
    count, extent, _, depth = inputs.shape
    stage["grad_in"] = jnp.transpose(unwritten((extent, extent, count, depth), BF16), (2, 0, 1, 3))
    lead = (((0,), (0,)), ((), ()))

    def chunk(n):
        slots = sizes[n]
        rows = slice(starts[n], starts[n] + slots)
        part = inputs[rows]
        e, slope = conv_forward(part, kernel, after(conv_bias[0]))
        pooled, inv = pool_forward(jnp.transpose(e, (1, 2, 0, 3)))
        last[0] = pooled
        partner_pool = swap_tower(pooled)
        yield
        rows_of = mix(after(pooled), partner_pool, self_pool, cross_pool, target, core, block)
        last[0] = rows_of[0]
        arrived = [rows_of[0]] + [swap_outer(r, k) for r, k in zip(rows_of[1:], order[1:])]
        yield
        arrived[0] = after(arrived[0])
        give = jnp.stack([r[1] for r in arrived])
        last[0] = give
        got = swap_core(give)
        yield
        chip, sent, flat = fc_forward(arrived, after(got), weight)
        last[0] = sent
        came = swap_core(sent)
        yield
        for hop in range(hops):
            chip, sent = halve(chip, after(came))
            last[0] = sent
            came = swap_outer(sent, 1 << hop)
            yield
        hiddens[n], gathered, bias_sum = hidden_step(
            n, chip, after(came), fc_bias[0], self_fc, cotangent[0], scaling, back_fc
        )
        sums["fc_bias"] += bias_sum[0]
        last[0] = gathered
        for hop in reversed(range(hops)):
            came = swap_outer(gathered, 1 << hop)
            yield
            gathered = jnp.concatenate([gathered, after(came)])
            last[0] = gathered
        came = swap_core(gathered)
        yield
        came = after(came)
        stage[n] = (flat, gathered, came)
        columns = fc_backward(gathered, came, weight)
        last[0] = columns[0]
        arrived = [columns[0]] + [swap_outer(c, k) for c, k in zip(columns[1:], order[1:])]
        yield
        arrived[0] = after(arrived[0])
        give = jnp.stack([r[1] for r in arrived])
        last[0] = give
        far = swap_core(give)
        yield
        grad_mixed, sent, stitch_sums = join(
            arrived, after(far), pooled, partner_pool, cross_pool, target, core, block
        )
        sums["pool"] += stitch_sums
        last[0] = sent
        back_pool = swap_tower(sent)
        yield
        grad_pre, bias_rows = pool_backward(
            jnp.transpose(slope, (1, 2, 0, 3)), grad_mixed, after(back_pool), inv, self_pool
        )
        sums["conv_bias"] += jnp.sum(bias_rows, axis=0)
        grad_pre = jnp.transpose(grad_pre, (2, 0, 1, 3))
        grad_kernel = conv_grad_kernel(part, grad_pre)
        sums["kernel"] += grad_kernel
        last[0] = grad_kernel
        yield
        part = conv_grad_inputs(after(grad_pre), kernel)
        stage["grad_in"] = lax.dynamic_update_slice(stage["grad_in"], part, (starts[n], 0, 0, 0))
        last[0] = stage["grad_in"]

    def stitch():
        hidden = after(jnp.concatenate([hiddens[n] for n in range(len(sizes))]))
        last[0] = hidden
        partner_hidden = swap_tower(hidden)
        yield
        partner_hidden = after(partner_hidden).astype(F32)
        hidden = hidden.astype(F32)
        stage["output"] = ((self_fc * hidden + cross_fc * partner_hidden) * live_slots[:, None]).astype(BF16)
        grad_out = cotangent[0].astype(F32) * scaling[:, None]
        stage["hidden"] = jnp.sum(hidden * grad_out, axis=0), jnp.sum(partner_hidden * grad_out, axis=0)
        last[0] = stage["output"]

    def fc_weight_gradient():
        columns = jnp.concatenate([stage[n][0] for n in range(len(sizes))])
        grads = after(jnp.concatenate([g.reshape(-1, units) for n in range(len(sizes)) for g in stage[n][1:]]))
        own, far = columns[:, :block], columns[:, block:]
        own, far = jnp.where(mid == 0, own, far), jnp.where(mid == 0, far, own)
        far_term = lax.dot_general(far, grads, lead, preferred_element_type=F32).astype(BF16)
        last[0] = far_term
        came = swap_mid(far_term)
        yield
        own, came = lax.optimization_barrier((own, after(came)))
        stage["gradient"] = lax.dot_general(own, grads, lead, preferred_element_type=F32) + came.astype(F32)
        last[0] = stage["gradient"]

    def kernel_sum():
        yield from sum_kernel(stage, last, after, sums["kernel"].reshape(-1, width), outer, mid, core)

    runs = {str(n): chunk(n) for n in range(len(sizes))}
    runs.update(W=fc_weight_gradient(), S=stitch(), A=kernel_sum())
    for n in PLAN if len(sizes) > 1 else "0" * (2 * hops + 6) + "WS" + "0" * 4 + "AA0" + "WS" + "A" * 5:
        next(runs[n], None)
    grad_fc_weight = stage["gradient"]
    conv_bias_sum, fc_bias_sum = sums["conv_bias"], sums["fc_bias"]
    hidden_self, hidden_cross = stage["hidden"]
    pool_self, pool_cross = sums["pool"]

    small = sum_small(
        jnp.concatenate([conv_bias_sum, pool_self, pool_cross, fc_bias_sum, hidden_self, hidden_cross])[None]
    )[0]
    cuts = [width, 2 * width, 3 * width, 3 * width + units, 3 * width + 2 * units]
    conv_bias_sum, pool_self, pool_cross, fc_bias_sum, hidden_self, hidden_cross = jnp.split(small, cuts)
    grad_row_pool = jnp.where(
        is_first, jnp.stack([pool_self, pool_cross]), jnp.stack([pool_cross, pool_self])
    )
    grad_row_fc = jnp.where(
        is_first, jnp.stack([hidden_self, hidden_cross]), jnp.stack([hidden_cross, hidden_self])
    )
    summed_kernel = stage["kernel"].reshape(kernel.shape)
    return (
        stage["output"][None],
        stage["grad_in"][None],
        summed_kernel[None],
        conv_bias_sum[None],
        grad_fc_weight[None],
        fc_bias_sum[None],
        grad_row_pool[None],
        grad_row_fc[None],
    )


def solution(mesh):
    mesh = jax.sharding.Mesh(mesh.devices.reshape(mesh.shape["tower"], -1, 2, 2), ("tower", "outer", "core", "mid"))
    crops = ("outer", "core", "mid")
    placed = (
        P("tower", crops, None, None, None),
        P("tower", None, None, None, None),
        P("tower", None),
        P("tower", crops, None),
        P("tower", None),
        P("tower", None, None),
        P("tower", None, None),
        P("tower", crops, None),
        P(crops),
        P(crops),
        P(crops),
    )
    return jax.shard_map(
        body,
        mesh=mesh,
        in_specs=placed,
        out_specs=(
            P("tower", crops, None),
            P("tower", crops, None, None, None),
            P("tower", None, None, None, None),
            P("tower", None),
            P("tower", crops, None),
            P("tower", None),
            P("tower", None, None),
            P("tower", None, None),
        ),
        check_vma=False,
    )
```

```python
import functools

import jax
import jax.numpy as jnp
from jax import lax
from jax.experimental import pallas as pl
from jax.experimental.pallas import tpu as pltpu
from jax.sharding import PartitionSpec as P

PLAN = ("0102010213012301320130210231301230210231", "S021302123W23W3S3AA1A2A3AAA")
BF16 = jnp.bfloat16
F32 = jnp.float32
CONV_DIMS = ("NHWC", "HWIO", "NHWC")
VMEM_LIMIT = 48 * 1024 * 1024


def swap_core(block):
    return lax.ppermute(block, "core", [(0, 1), (1, 0)])


def swap_mid(block):
    return lax.ppermute(block, "mid", [(0, 1), (1, 0)])


def swap_outer(block, mask):
    count = lax.axis_size("outer")
    return lax.ppermute(block, "outer", [(i, i ^ mask) for i in range(count)])


def swap_tower(block):
    return lax.ppermute(block, "tower", [(0, 1), (1, 0)])


def pick(stack, index):
    return lax.dynamic_index_in_dim(stack, index, 0, keepdims=False)


def pool_kernel(e_ref, pooled_ref, inv_ref):
    extent = e_ref.shape[0]
    width = e_ref.shape[3]
    out = (extent - 3) // 2 + 1

    def columns(row):
        cells = [e_ref[row, col].astype(F32) for col in range(extent)]
        return [cells[2 * j] + cells[2 * j + 1] + cells[2 * j + 2] for j in range(out)]

    top = columns(0)
    for i in range(out):
        middle = columns(2 * i + 1)
        bottom = columns(2 * i + 2)
        for j in range(out):
            total = top[j] + middle[j] + bottom[j]
            lanes = pl.ds((i * out + j) * width, width)
            pooled_ref[:, lanes] = jnp.log(total).astype(pooled_ref.dtype)
            inv_ref[:, lanes] = 2.0 / total
        top = bottom


def pool_forward(e):
    extent, _, slots, width = e.shape
    out = (extent - 3) // 2 + 1
    block = 16
    flat = out * out * width
    return pl.pallas_call(
        pool_kernel,
        grid=(slots // block,),
        in_specs=[pl.BlockSpec((extent, extent, block, width), lambda s: (0, 0, s, 0))],
        out_specs=[
            pl.BlockSpec((block, flat), lambda s: (s, 0)),
            pl.BlockSpec((block, flat), lambda s: (s, 0)),
        ],
        out_shape=[
            jax.ShapeDtypeStruct((slots, flat), BF16),
            jax.ShapeDtypeStruct((slots, flat), F32),
        ],
        compiler_params=pltpu.CompilerParams(vmem_limit_bytes=VMEM_LIMIT),
        cost_estimate=pl.CostEstimate(flops=0, bytes_accessed=0, transcendentals=0),
        name="pool_forward",
    )(e)


def pool_back_kernel(slope_ref, grad_ref, back_ref, inv_ref, self_ref, g_ref, bias_ref):
    extent = slope_ref.shape[0]
    width = slope_ref.shape[3]
    out = (extent - 3) // 2 + 1
    coef = self_ref[0:1, :]

    @pl.when(pl.program_id(0) == 0)
    def _():
        bias_ref[...] = jnp.zeros_like(bias_ref)

    def window_row(i):
        row = []
        for j in range(out):
            lanes = pl.ds((i * out + j) * width, width)
            grad = coef * grad_ref[:, lanes].astype(F32) + back_ref[:, lanes].astype(F32)
            row.append(grad * inv_ref[:, lanes])
        return row

    sums = jnp.zeros((slope_ref.shape[2], width), F32)
    above = None
    current = window_row(0)
    for row in range(extent):
        if row % 2 == 0:
            if row == 0:
                rows = current
            elif row == extent - 1:
                rows = current
            else:
                above, current = current, window_row(row // 2)
                rows = [a + b for a, b in zip(above, current)]
        else:
            rows = current
        for col in range(extent):
            if col % 2 == 1:
                spread = rows[col // 2]
            elif col == 0:
                spread = rows[0]
            elif col == extent - 1:
                spread = rows[out - 1]
            else:
                spread = rows[col // 2 - 1] + rows[col // 2]
            grad = (slope_ref[row, col].astype(F32) * spread).astype(g_ref.dtype)
            g_ref[row, col] = grad
            sums = sums + grad.astype(F32)
    bias_ref[...] += sums


def pool_backward(slope, grad_mixed, back_pool, inv, self_pool):
    extent, _, slots, width = slope.shape
    block = 16
    flat = grad_mixed.shape[1]
    rows = pl.BlockSpec((block, flat), lambda s: (s, 0))
    grid_block = pl.BlockSpec((extent, extent, block, width), lambda s: (0, 0, s, 0))
    return pl.pallas_call(
        pool_back_kernel,
        grid=(slots // block,),
        in_specs=[grid_block, rows, rows, rows, pl.BlockSpec((1, width), lambda s: (0, 0))],
        out_specs=[grid_block, pl.BlockSpec((block, width), lambda s: (0, 0))],
        out_shape=[
            jax.ShapeDtypeStruct(slope.shape, BF16),
            jax.ShapeDtypeStruct((block, width), F32),
        ],
        compiler_params=pltpu.CompilerParams(vmem_limit_bytes=VMEM_LIMIT),
        cost_estimate=pl.CostEstimate(flops=0, bytes_accessed=0, transcendentals=0),
        name="pool_backward",
    )(slope, grad_mixed, back_pool, inv, self_pool[None])


def mix_kernel(block, target_ref, core_ref, pooled_ref, partner_ref, self_ref, cross_ref, *out_refs):
    reach = 4 * block
    is_zero = core_ref[0] == 0
    for p, out_ref in enumerate(out_refs):
        lanes = pl.ds(pl.multiple_of(target_ref[p] * reach, 128), reach)
        mixed = self_ref[...] * pooled_ref[:, lanes].astype(F32) + cross_ref[...] * partner_ref[:, lanes].astype(F32)
        first = mixed[:, : 2 * block]
        second = mixed[:, 2 * block :]
        out_ref[0] = jnp.where(is_zero, first, second).astype(out_ref.dtype)
        out_ref[1] = jnp.where(is_zero, second, first).astype(out_ref.dtype)


def mix(pooled, partner_pool, self_pool, cross_pool, target, core, block):
    slots, flat = pooled.shape
    count = flat // (4 * block)
    shape = jax.ShapeDtypeStruct((2, slots, 2 * block), BF16)
    if (4 * block) % 128:
        width = self_pool.shape[0]
        mixed = (
            jnp.tile(self_pool, flat // width) * pooled.astype(F32)
            + jnp.tile(cross_pool, flat // width) * partner_pool.astype(F32)
        ).astype(BF16)
        mixed = mixed.reshape(slots, count, 2, 2, block).transpose(1, 2, 0, 3, 4).reshape(count, 2, slots, 2 * block)
        mixed = jnp.where(core == 0, mixed, mixed[:, ::-1])
        return [pick(mixed, target[p]) for p in range(count)]
    repeat = 4 * block // self_pool.shape[0]
    smem = pl.BlockSpec(memory_space=pltpu.SMEM)
    vmem = pl.BlockSpec(memory_space=pltpu.VMEM)
    return pl.pallas_call(
        functools.partial(mix_kernel, block),
        in_specs=[smem, smem, vmem, vmem, vmem, vmem],
        out_specs=[vmem] * count,
        out_shape=[shape] * count,
        compiler_params=pltpu.CompilerParams(vmem_limit_bytes=VMEM_LIMIT),
        cost_estimate=pl.CostEstimate(flops=0, bytes_accessed=0, transcendentals=0),
        name="mix",
    )(target, core[None], pooled, partner_pool, jnp.tile(self_pool, repeat)[None], jnp.tile(cross_pool, repeat)[None])


def join_kernel(block, count, width, target_ref, core_ref, cross_ref, pooled_ref, partner_ref, far_ref, *refs):
    here_refs = refs[:count]
    grad_ref, sent_ref, sums_ref = refs[count:]
    reach = 4 * block
    is_zero = core_ref[0] == 0
    own_sum = jnp.zeros((1, reach), F32)
    cross_sum = jnp.zeros((1, reach), F32)
    for p in range(count):
        lanes = pl.ds(pl.multiple_of(target_ref[p] * reach, 128), reach)
        here, there = here_refs[p][0].astype(F32), far_ref[p].astype(F32)
        zero, one = jnp.where(is_zero, here, there), jnp.where(is_zero, there, here)
        grad = jnp.concatenate([zero, one], axis=1)
        grad_ref[:, lanes] = grad.astype(grad_ref.dtype)
        sent_ref[:, lanes] = (cross_ref[...] * grad).astype(sent_ref.dtype)
        own_sum = own_sum + jnp.sum(pooled_ref[:, lanes].astype(F32) * grad, axis=0, keepdims=True)
        cross_sum = cross_sum + jnp.sum(partner_ref[:, lanes].astype(F32) * grad, axis=0, keepdims=True)
    for row, total in enumerate((own_sum, cross_sum)):
        folded = total[:, :width]
        for cell in range(1, reach // width):
            folded = folded + total[:, cell * width : (cell + 1) * width]
        sums_ref[row : row + 1, :] = folded


def join(here, far, pooled, partner_pool, cross_pool, target, core, block):
    slots, flat = pooled.shape
    count = flat // (4 * block)
    width = cross_pool.shape[0]
    if (4 * block) % 128:
        pieces = jnp.stack([jnp.stack([here[p][0], far[p]]) for p in range(count)])
        pieces = jnp.where(core == 0, pieces, pieces[:, ::-1]).reshape(count, 2, slots, 2, block)
        inverse = jnp.argsort(target)
        grad = jnp.take(pieces, inverse, axis=0).transpose(2, 0, 1, 3, 4).reshape(slots, flat)
        wide = grad.astype(F32)
        sent = (jnp.tile(cross_pool, flat // width) * wide).astype(BF16)
        sums = [
            jnp.sum(jnp.sum(a.astype(F32) * wide, axis=0).reshape(-1, width), axis=0) for a in (pooled, partner_pool)
        ]
        return grad, sent, jnp.stack(sums)
    smem = pl.BlockSpec(memory_space=pltpu.SMEM)
    vmem = pl.BlockSpec(memory_space=pltpu.VMEM)
    return pl.pallas_call(
        functools.partial(join_kernel, block, count, width),
        in_specs=[smem, smem] + [vmem] * (4 + count),
        out_specs=[vmem] * 3,
        out_shape=[
            jax.ShapeDtypeStruct((slots, flat), BF16),
            jax.ShapeDtypeStruct((slots, flat), BF16),
            jax.ShapeDtypeStruct((2, width), F32),
        ],
        compiler_params=pltpu.CompilerParams(vmem_limit_bytes=VMEM_LIMIT),
        cost_estimate=pl.CostEstimate(flops=0, bytes_accessed=0, transcendentals=0),
        name="join",
    )(target, core[None], jnp.tile(cross_pool, 4 * block // width)[None], pooled, partner_pool, far, *here)


def fc_forward_kernel(count, w_ref, got_ref, *refs):
    row_refs = refs[:count]
    chip_ref, sent_ref, all_ref = refs[count:]
    slots = got_ref.shape[1]

    @pl.when(pl.program_id(0) == 0)
    def _():
        for p in range(count):
            all_ref[pl.ds(p * slots, slots), :] = row_refs[p][0]
            all_ref[pl.ds((count + p) * slots, slots), :] = got_ref[p]

    total = jnp.dot(all_ref[...], w_ref[...], preferred_element_type=F32)
    half = count * slots
    for p in range(count):
        chip_ref[p] = total[p * slots : (p + 1) * slots]
        sent_ref[p] = total[half + p * slots : half + (p + 1) * slots].astype(sent_ref.dtype)


def fc_forward(rows, got, weight):
    count, (slots, depth), units = len(rows), got.shape[1:], weight.shape[1]
    tile = 1024
    if count > 4:
        used = jnp.concatenate([r[0] for r in rows] + [got.reshape(-1, depth)])
        total = jnp.dot(used, weight, preferred_element_type=F32).reshape(2, count, slots, units)
        return total[0], total[1].astype(BF16), used
    mine = pl.BlockSpec((1, slots, depth), lambda t: (0, 0, 0))
    out = pl.BlockSpec((count, slots, tile), lambda t: (0, 0, t))
    size = 2 * count * slots
    return pl.pallas_call(
        functools.partial(fc_forward_kernel, count),
        grid=(units // tile,),
        in_specs=[
            pl.BlockSpec((depth, tile), lambda t: (0, t)),
            pl.BlockSpec((count, slots, depth), lambda t: (0, 0, 0)),
        ]
        + [mine] * count,
        out_specs=[out, out, pl.BlockSpec((size, depth), lambda t: (0, 0))],
        out_shape=[
            jax.ShapeDtypeStruct((count, slots, units), F32),
            jax.ShapeDtypeStruct((count, slots, units), BF16),
            jax.ShapeDtypeStruct((size, depth), BF16),
        ],
        compiler_params=pltpu.CompilerParams(vmem_limit_bytes=VMEM_LIMIT),
        cost_estimate=pl.CostEstimate(flops=0, bytes_accessed=0, transcendentals=0),
        name="fc_forward",
    )(weight, got, *rows)


def fc_back_kernel(count, w_ref, own_ref, came_ref, *refs):
    out_refs, grads_ref = refs[:count], refs[count]
    slots, units = own_ref.shape[1:]
    half = count * slots

    @pl.when(pl.program_id(0) == 0)
    def _():
        grads_ref[:half] = own_ref[...].reshape(half, units)
        grads_ref[half:] = came_ref[...].reshape(half, units)

    total = lax.dot_general(grads_ref[...], w_ref[...], (((1,), (1,)), ((), ())), preferred_element_type=F32)
    for p, out_ref in enumerate(out_refs):
        for side in range(2):
            first = side * half + p * slots
            out_ref[side] = total[first : first + slots].astype(out_ref.dtype)


def fc_backward(own, came, weight):
    count, slots, units = own.shape
    depth = weight.shape[0]
    tile = 384 if depth % 384 == 0 else depth
    if count > 4:
        grads = jnp.stack([own, came], axis=1).reshape(-1, units)
        columns = lax.dot_general(grads, weight, (((1,), (1,)), ((), ())), preferred_element_type=F32)
        columns = columns.astype(BF16).reshape(count, 2, slots, depth)
        return [columns[p] for p in range(count)]
    grads = pl.BlockSpec((count, slots, units), lambda t: (0, 0, 0))
    return pl.pallas_call(
        functools.partial(fc_back_kernel, count),
        grid=(depth // tile,),
        in_specs=[pl.BlockSpec((tile, units), lambda t: (t, 0)), grads, grads],
        out_specs=[pl.BlockSpec((2, slots, tile), lambda t: (0, 0, t))] * count,
        out_shape=[jax.ShapeDtypeStruct((2, slots, depth), BF16)] * count,
        scratch_shapes=[pltpu.VMEM((2 * count * slots, units), BF16)],
        compiler_params=pltpu.CompilerParams(vmem_limit_bytes=VMEM_LIMIT),
        cost_estimate=pl.CostEstimate(flops=0, bytes_accessed=0, transcendentals=0),
        name="fc_backward",
    )(weight, own, came)


def halve_kernel(kept_ref, came_ref, out_ref, sent_ref):
    total = kept_ref[...] + came_ref[...].astype(F32)
    half = out_ref.shape[0]
    out_ref[...] = total[:half]
    sent_ref[...] = total[half:].astype(sent_ref.dtype)


def halve(kept, came):
    count, slots, units = kept.shape
    half = count // 2
    if count > 4:
        total = kept + came.astype(F32)
        return total[:half], total[half:].astype(BF16)
    tile = units // 4
    return pl.pallas_call(
        halve_kernel,
        grid=(4,),
        in_specs=[pl.BlockSpec((count, slots, tile), lambda t: (0, 0, t))] * 2,
        out_specs=[pl.BlockSpec((half, slots, tile), lambda t: (0, 0, t))] * 2,
        out_shape=[
            jax.ShapeDtypeStruct((half, slots, units), F32),
            jax.ShapeDtypeStruct((half, slots, units), BF16),
        ],
        compiler_params=pltpu.CompilerParams(vmem_limit_bytes=VMEM_LIMIT),
        cost_estimate=pl.CostEstimate(flops=0, bytes_accessed=0, transcendentals=0),
        name="halve",
    )(kept, came)


def hidden_kernel(kept_ref, came_ref, bias_ref, self_ref, cot_ref, scale_ref, back_ref, hidden_ref, grad_ref, sum_ref):
    pre = kept_ref[0] + came_ref[0].astype(F32) + bias_ref[...]
    hidden, slope = gelu_parts(pre)
    hidden_ref[...] = hidden.astype(hidden_ref.dtype)
    grad_out = cot_ref[...].astype(F32) * scale_ref[...]
    grad = ((self_ref[...] * grad_out + back_ref[...].astype(F32)) * slope).astype(grad_ref.dtype)
    grad_ref[0] = grad
    sum_ref[...] = jnp.sum(grad.astype(F32), axis=0, keepdims=True)


def hidden_step(n, kept, came, bias, self_fc, cotangent, scaling, back_fc):
    _, slots, units = kept.shape
    tile = units // 4
    one = pl.BlockSpec((1, tile), lambda t: (0, t))
    block = pl.BlockSpec((1, slots, tile), lambda t: (0, 0, t))
    rows = pl.BlockSpec((slots, tile), lambda t: (n, t))
    return pl.pallas_call(
        hidden_kernel,
        grid=(4,),
        in_specs=[block, block, one, one, rows, pl.BlockSpec((slots, 1), lambda t: (n, 0)), rows],
        out_specs=[pl.BlockSpec((slots, tile), lambda t: (0, t)), block, one],
        out_shape=[
            jax.ShapeDtypeStruct((slots, units), BF16),
            jax.ShapeDtypeStruct((1, slots, units), BF16),
            jax.ShapeDtypeStruct((1, units), F32),
        ],
        compiler_params=pltpu.CompilerParams(vmem_limit_bytes=VMEM_LIMIT),
        cost_estimate=pl.CostEstimate(flops=0, bytes_accessed=0, transcendentals=0),
        name="hidden",
    )(kept, came, bias[None], self_fc[None], cotangent, scaling[:, None], back_fc)


def unwritten(shape, dtype):
    return pl.pallas_call(
        lambda ref: None,
        out_specs=pl.BlockSpec(memory_space=pl.ANY),
        out_shape=jax.ShapeDtypeStruct(shape, dtype),
        cost_estimate=pl.CostEstimate(flops=0, bytes_accessed=0, transcendentals=0),
        name="unwritten",
    )()


def gelu_parts(v):
    root = 0.7978845608028654
    cubic = 0.044715
    square = v * v
    half = 0.5 + 0.5 * jnp.tanh(v * (root + (root * cubic) * square))
    slope = half + (half * (1.0 - half)) * (v * (2.0 * root + (6.0 * root * cubic) * square))
    return v * half, slope


def conv_forward(inputs, kernel, bias):
    pre_conv = lax.conv_general_dilated(
        inputs, kernel, (1, 1), ((1, 1), (1, 1)), dimension_numbers=CONV_DIMS, preferred_element_type=F32
    )
    activity, slope = gelu_parts(pre_conv + bias)
    e = jnp.exp(activity)
    return e.astype(BF16), ((0.5 * e) * slope).astype(BF16)


def conv_grad_inputs(grad_pre, kernel):
    turned = jnp.flip(kernel, (0, 1)).swapaxes(2, 3)
    return lax.conv_general_dilated(
        grad_pre, turned, (1, 1), ((1, 1), (1, 1)), dimension_numbers=CONV_DIMS, preferred_element_type=F32
    ).astype(BF16)


def conv_grad_kernel(inputs, grad_pre):
    dims = lax.ConvDimensionNumbers(lhs_spec=(3, 0, 1, 2), rhs_spec=(3, 0, 1, 2), out_spec=(2, 3, 0, 1))
    return lax.conv_general_dilated(
        inputs, grad_pre, (1, 1), ((1, 1), (1, 1)), dimension_numbers=dims, preferred_element_type=F32
    )


def sum_small(vector):
    vector = vector + swap_core(vector)
    vector = vector + swap_mid(vector)
    step = 1
    while step < lax.axis_size("outer"):
        vector = vector + swap_outer(vector, step)
        step *= 2
    return vector


def sum_kernel(stage, last, after, rows, outer, mid, core):
    outer_count = lax.axis_size("outer")
    for swap, side in ((swap_mid, mid), (swap_core, core)):
        halves = rows.reshape(2, -1, rows.shape[1])
        sent, kept = pick(halves, 1 - side).astype(BF16), pick(halves, side)
        last[0] = sent
        got = swap(sent)
        yield
        rows = kept + after(got).astype(F32)
    parts = rows.reshape(outer_count, -1, rows.shape[1])
    total = pick(parts, outer)
    sent = [pick(parts, outer ^ k).astype(BF16) for k in range(1, outer_count)]
    last[0] = sent[-1]
    got = [swap_outer(s, k + 1) for k, s in enumerate(sent)]
    yield
    got[0] = after(got[0])
    for g in got:
        total = total + g.astype(F32)
    total = total.astype(BF16)
    last[0] = total
    stack = [total] + [swap_outer(total, k) for k in range(1, outer_count)]
    yield
    stack = jnp.stack([after(total), *stack[1:]])
    rows = jnp.concatenate([pick(stack, outer ^ k) for k in range(outer_count)])
    for swap, side in ((swap_core, core), (swap_mid, mid)):
        last[0] = rows
        got = swap(rows)
        yield
        got = after(got)
        rows = jnp.where(side == 0, jnp.concatenate([rows, got]), jnp.concatenate([got, rows]))
    stage["kernel"] = rows.astype(F32)


def body(
    features,
    conv_weight,
    conv_bias,
    fc_weight,
    fc_bias,
    stitch_pool,
    stitch_fc,
    cotangent,
    crop_counts,
    slot_image,
    slot_mask,
):
    is_first = lax.axis_index("tower") == 0
    core, mid, outer = lax.axis_index("core"), lax.axis_index("mid"), lax.axis_index("outer")
    outer_count = lax.axis_size("outer")
    block, units = fc_weight.shape[1:]
    weight = lax.all_gather(fc_weight[0], "mid", axis=0, tiled=True)

    row_pool = stitch_pool[0]
    self_pool = jnp.where(is_first, row_pool[0], row_pool[1])
    cross_pool = jnp.where(is_first, row_pool[1], row_pool[0])
    row_fc = stitch_fc[0]
    self_fc = jnp.where(is_first, row_fc[0], row_fc[1])
    cross_fc = jnp.where(is_first, row_fc[1], row_fc[0])

    live_slots = slot_mask.astype(F32)
    image_ids = jnp.arange(crop_counts.shape[0], dtype=jnp.int32)
    matches = (slot_image[:, None] == image_ids[None, :]).astype(F32)
    per_slot = jnp.sum(matches * crop_counts.astype(F32)[None, :], axis=1)
    scaling = live_slots / per_slot
    sent_fc = (cross_fc * (cotangent[0].astype(F32) * scaling[:, None])).astype(BF16)
    back_fc = swap_tower(sent_fc)

    inputs = features[0]
    kernel = conv_weight[0]
    width = kernel.shape[3]
    hops = outer_count.bit_length() - 1
    order = [sum(((p >> b) & 1) << (hops - 1 - b) for b in range(hops)) for p in range(outer_count)]
    target = outer ^ jnp.array(order, jnp.int32)
    total_slots = inputs.shape[0]
    sizes = [total_slots // 4] * 4 if outer_count <= 4 else [total_slots]
    starts = [sum(sizes[:n]) for n in range(len(sizes))]
    last = [scaling]

    def after(array):
        return lax.optimization_barrier((array, last[0]))[0]

    sums = dict(fc_bias=0.0, pool=0.0, conv_bias=0.0, kernel=0.0)
    stage = {}
    hiddens = {}
    count, extent, _, depth = inputs.shape
    stage["grad_in"] = jnp.transpose(unwritten((extent, extent, count, depth), BF16), (2, 0, 1, 3))
    lead = (((0,), (0,)), ((), ()))

    def chunk(n):
        slots = sizes[n]
        rows = slice(starts[n], starts[n] + slots)
        part = inputs[rows]
        e, slope = conv_forward(part, kernel, after(conv_bias[0]))
        pooled, inv = pool_forward(jnp.transpose(e, (1, 2, 0, 3)))
        last[0] = pooled
        partner_pool = swap_tower(pooled)
        yield
        rows_of = mix(after(pooled), partner_pool, self_pool, cross_pool, target, core, block)
        last[0] = rows_of[0]
        arrived = [rows_of[0]] + [swap_outer(r, k) for r, k in zip(rows_of[1:], order[1:])]
        yield
        arrived[0] = after(arrived[0])
        give = jnp.stack([r[1] for r in arrived])
        last[0] = give
        got = swap_core(give)
        yield
        chip, sent, flat = fc_forward(arrived, after(got), weight)
        last[0] = sent
        came = swap_core(sent)
        yield
        for hop in range(hops):
            chip, sent = halve(chip, after(came))
            last[0] = sent
            came = swap_outer(sent, 1 << hop)
            yield
        hiddens[n], gathered, bias_sum = hidden_step(
            n, chip, after(came), fc_bias[0], self_fc, cotangent[0], scaling, back_fc
        )
        sums["fc_bias"] += bias_sum[0]
        last[0] = gathered
        for hop in reversed(range(hops)):
            came = swap_outer(gathered, 1 << hop)
            yield
            gathered = jnp.concatenate([gathered, after(came)])
            last[0] = gathered
        came = swap_core(gathered)
        yield
        came = after(came)
        stage[n] = (flat, gathered, came)
        columns = fc_backward(gathered, came, weight)
        last[0] = columns[0]
        arrived = [columns[0]] + [swap_outer(c, k) for c, k in zip(columns[1:], order[1:])]
        yield
        arrived[0] = after(arrived[0])
        give = jnp.stack([r[1] for r in arrived])
        last[0] = give
        far = swap_core(give)
        yield
        grad_mixed, sent, stitch_sums = join(
            arrived, after(far), pooled, partner_pool, cross_pool, target, core, block
        )
        sums["pool"] += stitch_sums
        last[0] = sent
        back_pool = swap_tower(sent)
        yield
        grad_pre, bias_rows = pool_backward(
            jnp.transpose(slope, (1, 2, 0, 3)), grad_mixed, after(back_pool), inv, self_pool
        )
        sums["conv_bias"] += jnp.sum(bias_rows, axis=0)
        grad_pre = jnp.transpose(grad_pre, (2, 0, 1, 3))
        grad_kernel = conv_grad_kernel(part, grad_pre)
        sums["kernel"] += grad_kernel
        last[0] = grad_kernel
        yield
        part = conv_grad_inputs(after(grad_pre), kernel)
        stage["grad_in"] = lax.dynamic_update_slice(stage["grad_in"], part, (starts[n], 0, 0, 0))
        last[0] = stage["grad_in"]

    def stitch():
        hidden = after(jnp.concatenate([hiddens[n] for n in range(len(sizes))]))
        last[0] = hidden
        partner_hidden = swap_tower(hidden)
        yield
        partner_hidden = after(partner_hidden).astype(F32)
        hidden = hidden.astype(F32)
        stage["output"] = ((self_fc * hidden + cross_fc * partner_hidden) * live_slots[:, None]).astype(BF16)
        grad_out = cotangent[0].astype(F32) * scaling[:, None]
        stage["hidden"] = jnp.sum(hidden * grad_out, axis=0), jnp.sum(partner_hidden * grad_out, axis=0)
        last[0] = stage["output"]

    def fc_weight_gradient():
        columns = jnp.concatenate([stage[n][0] for n in range(len(sizes))])
        grads = after(jnp.concatenate([g.reshape(-1, units) for n in range(len(sizes)) for g in stage[n][1:]]))
        own, far = columns[:, :block], columns[:, block:]
        own, far = jnp.where(mid == 0, own, far), jnp.where(mid == 0, far, own)
        far_term = lax.dot_general(far, grads, lead, preferred_element_type=F32).astype(BF16)
        last[0] = far_term
        came = swap_mid(far_term)
        yield
        own, came = lax.optimization_barrier((own, after(came)))
        stage["gradient"] = lax.dot_general(own, grads, lead, preferred_element_type=F32) + came.astype(F32)
        last[0] = stage["gradient"]

    def kernel_sum():
        yield from sum_kernel(stage, last, after, sums["kernel"].reshape(-1, width), outer, mid, core)

    runs = {str(n): chunk(n) for n in range(len(sizes))}
    runs.update(W=fc_weight_gradient(), S=stitch(), A=kernel_sum())
    for n in "".join(PLAN) if len(sizes) > 1 else "0" * (2 * hops + 6) + "WS" + "0" * 4 + "AA0" + "WS" + "A" * 5:
        next(runs[n], None)
    grad_fc_weight = stage["gradient"]
    conv_bias_sum, fc_bias_sum = sums["conv_bias"], sums["fc_bias"]
    hidden_self, hidden_cross = stage["hidden"]
    pool_self, pool_cross = sums["pool"]

    small = sum_small(
        jnp.concatenate([conv_bias_sum, pool_self, pool_cross, fc_bias_sum, hidden_self, hidden_cross])[None]
    )[0]
    cuts = [width, 2 * width, 3 * width, 3 * width + units, 3 * width + 2 * units]
    conv_bias_sum, pool_self, pool_cross, fc_bias_sum, hidden_self, hidden_cross = jnp.split(small, cuts)
    grad_row_pool = jnp.where(
        is_first, jnp.stack([pool_self, pool_cross]), jnp.stack([pool_cross, pool_self])
    )
    grad_row_fc = jnp.where(
        is_first, jnp.stack([hidden_self, hidden_cross]), jnp.stack([hidden_cross, hidden_self])
    )
    summed_kernel = stage["kernel"].reshape(kernel.shape)
    return (
        stage["output"][None],
        stage["grad_in"][None],
        summed_kernel[None],
        conv_bias_sum[None],
        grad_fc_weight[None],
        fc_bias_sum[None],
        grad_row_pool[None],
        grad_row_fc[None],
    )


def solution(mesh):
    mesh = jax.sharding.Mesh(mesh.devices.reshape(mesh.shape["tower"], -1, 2, 2), ("tower", "outer", "core", "mid"))
    crops = ("outer", "core", "mid")
    placed = (
        P("tower", crops, None, None, None),
        P("tower", None, None, None, None),
        P("tower", None),
        P("tower", crops, None),
        P("tower", None),
        P("tower", None, None),
        P("tower", None, None),
        P("tower", crops, None),
        P(crops),
        P(crops),
        P(crops),
    )
    return jax.shard_map(
        body,
        mesh=mesh,
        in_specs=placed,
        out_specs=(
            P("tower", crops, None),
            P("tower", crops, None, None, None),
            P("tower", None, None, None, None),
            P("tower", None),
            P("tower", crops, None),
            P("tower", None),
            P("tower", None, None),
            P("tower", None, None),
        ),
        check_vma=False,
    )
```

```python
import functools

import jax
import jax.numpy as jnp
from jax import lax
from jax.experimental import pallas as pl
from jax.experimental.pallas import tpu as pltpu
from jax.sharding import PartitionSpec as P

PLAN = ("0102010213012301320130210231301230210231", "S021302123W23W3S3AA1A2A3AAA")
BF16 = jnp.bfloat16
F32 = jnp.float32
CONV_DIMS = ("NHWC", "HWIO", "NHWC")
VMEM_LIMIT = 48 * 1024 * 1024


def swap_core(block):
    return lax.ppermute(block, "core", [(0, 1), (1, 0)])


def swap_mid(block):
    return lax.ppermute(block, "mid", [(0, 1), (1, 0)])


def swap_outer(block, mask):
    count = lax.axis_size("outer")
    return lax.ppermute(block, "outer", [(i, i ^ mask) for i in range(count)])


def swap_tower(block):
    return lax.ppermute(block, "tower", [(0, 1), (1, 0)])


def pick(stack, index):
    return lax.dynamic_index_in_dim(stack, index, 0, keepdims=False)


def pool_kernel(e_ref, pooled_ref, inv_ref):
    extent = e_ref.shape[0]
    width = e_ref.shape[3]
    out = (extent - 3) // 2 + 1

    def columns(row):
        cells = [e_ref[row, col].astype(F32) for col in range(extent)]
        return [cells[2 * j] + cells[2 * j + 1] + cells[2 * j + 2] for j in range(out)]

    top = columns(0)
    for i in range(out):
        middle = columns(2 * i + 1)
        bottom = columns(2 * i + 2)
        for j in range(out):
            total = top[j] + middle[j] + bottom[j]
            lanes = pl.ds((i * out + j) * width, width)
            pooled_ref[:, lanes] = jnp.log(total).astype(pooled_ref.dtype)
            inv_ref[:, lanes] = 2.0 / total
        top = bottom


def pool_forward(e):
    extent, _, slots, width = e.shape
    out = (extent - 3) // 2 + 1
    block = 16
    flat = out * out * width
    return pl.pallas_call(
        pool_kernel,
        grid=(slots // block,),
        in_specs=[pl.BlockSpec((extent, extent, block, width), lambda s: (0, 0, s, 0))],
        out_specs=[
            pl.BlockSpec((block, flat), lambda s: (s, 0)),
            pl.BlockSpec((block, flat), lambda s: (s, 0)),
        ],
        out_shape=[
            jax.ShapeDtypeStruct((slots, flat), BF16),
            jax.ShapeDtypeStruct((slots, flat), F32),
        ],
        compiler_params=pltpu.CompilerParams(vmem_limit_bytes=VMEM_LIMIT),
        cost_estimate=pl.CostEstimate(flops=0, bytes_accessed=0, transcendentals=0),
        name="pool_forward",
    )(e)


def pool_back_kernel(slope_ref, grad_ref, back_ref, inv_ref, self_ref, g_ref, bias_ref):
    extent = slope_ref.shape[0]
    width = slope_ref.shape[3]
    out = (extent - 3) // 2 + 1
    coef = self_ref[0:1, :]

    @pl.when(pl.program_id(0) == 0)
    def _():
        bias_ref[...] = jnp.zeros_like(bias_ref)

    def window_row(i):
        row = []
        for j in range(out):
            lanes = pl.ds((i * out + j) * width, width)
            grad = coef * grad_ref[:, lanes].astype(F32) + back_ref[:, lanes].astype(F32)
            row.append(grad * inv_ref[:, lanes])
        return row

    sums = jnp.zeros((slope_ref.shape[2], width), F32)
    above = None
    current = window_row(0)
    for row in range(extent):
        if row % 2 == 0:
            if row == 0:
                rows = current
            elif row == extent - 1:
                rows = current
            else:
                above, current = current, window_row(row // 2)
                rows = [a + b for a, b in zip(above, current)]
        else:
            rows = current
        for col in range(extent):
            if col % 2 == 1:
                spread = rows[col // 2]
            elif col == 0:
                spread = rows[0]
            elif col == extent - 1:
                spread = rows[out - 1]
            else:
                spread = rows[col // 2 - 1] + rows[col // 2]
            grad = (slope_ref[row, col].astype(F32) * spread).astype(g_ref.dtype)
            g_ref[row, col] = grad
            sums = sums + grad.astype(F32)
    bias_ref[...] += sums


def pool_backward(slope, grad_mixed, back_pool, inv, self_pool):
    extent, _, slots, width = slope.shape
    block = 16
    flat = grad_mixed.shape[1]
    rows = pl.BlockSpec((block, flat), lambda s: (s, 0))
    grid_block = pl.BlockSpec((extent, extent, block, width), lambda s: (0, 0, s, 0))
    return pl.pallas_call(
        pool_back_kernel,
        grid=(slots // block,),
        in_specs=[grid_block, rows, rows, rows, pl.BlockSpec((1, width), lambda s: (0, 0))],
        out_specs=[grid_block, pl.BlockSpec((block, width), lambda s: (0, 0))],
        out_shape=[
            jax.ShapeDtypeStruct(slope.shape, BF16),
            jax.ShapeDtypeStruct((block, width), F32),
        ],
        compiler_params=pltpu.CompilerParams(vmem_limit_bytes=VMEM_LIMIT),
        cost_estimate=pl.CostEstimate(flops=0, bytes_accessed=0, transcendentals=0),
        name="pool_backward",
    )(slope, grad_mixed, back_pool, inv, self_pool[None])


def mix_kernel(block, target_ref, core_ref, pooled_ref, partner_ref, self_ref, cross_ref, *out_refs):
    reach = 4 * block
    is_zero = core_ref[0] == 0
    for p, out_ref in enumerate(out_refs):
        lanes = pl.ds(pl.multiple_of(target_ref[p] * reach, 128), reach)
        mixed = self_ref[...] * pooled_ref[:, lanes].astype(F32) + cross_ref[...] * partner_ref[:, lanes].astype(F32)
        first = mixed[:, : 2 * block]
        second = mixed[:, 2 * block :]
        out_ref[0] = jnp.where(is_zero, first, second).astype(out_ref.dtype)
        out_ref[1] = jnp.where(is_zero, second, first).astype(out_ref.dtype)


def mix(pooled, partner_pool, self_pool, cross_pool, target, core, block):
    slots, flat = pooled.shape
    count = flat // (4 * block)
    shape = jax.ShapeDtypeStruct((2, slots, 2 * block), BF16)
    if (4 * block) % 128:
        width = self_pool.shape[0]
        mixed = (
            jnp.tile(self_pool, flat // width) * pooled.astype(F32)
            + jnp.tile(cross_pool, flat // width) * partner_pool.astype(F32)
        ).astype(BF16)
        mixed = mixed.reshape(slots, count, 2, 2, block).transpose(1, 2, 0, 3, 4).reshape(count, 2, slots, 2 * block)
        mixed = jnp.where(core == 0, mixed, mixed[:, ::-1])
        return [pick(mixed, target[p]) for p in range(count)]
    repeat = 4 * block // self_pool.shape[0]
    smem = pl.BlockSpec(memory_space=pltpu.SMEM)
    vmem = pl.BlockSpec(memory_space=pltpu.VMEM)
    return pl.pallas_call(
        functools.partial(mix_kernel, block),
        in_specs=[smem, smem, vmem, vmem, vmem, vmem],
        out_specs=[vmem] * count,
        out_shape=[shape] * count,
        compiler_params=pltpu.CompilerParams(vmem_limit_bytes=VMEM_LIMIT),
        cost_estimate=pl.CostEstimate(flops=0, bytes_accessed=0, transcendentals=0),
        name="mix",
    )(target, core[None], pooled, partner_pool, jnp.tile(self_pool, repeat)[None], jnp.tile(cross_pool, repeat)[None])


def join_kernel(block, count, width, target_ref, core_ref, cross_ref, pooled_ref, partner_ref, far_ref, *refs):
    here_refs = refs[:count]
    grad_ref, sent_ref, sums_ref = refs[count:]
    reach = 4 * block
    is_zero = core_ref[0] == 0
    own_sum = jnp.zeros((1, reach), F32)
    cross_sum = jnp.zeros((1, reach), F32)
    for p in range(count):
        lanes = pl.ds(pl.multiple_of(target_ref[p] * reach, 128), reach)
        here, there = here_refs[p][0].astype(F32), far_ref[p].astype(F32)
        zero, one = jnp.where(is_zero, here, there), jnp.where(is_zero, there, here)
        grad = jnp.concatenate([zero, one], axis=1)
        grad_ref[:, lanes] = grad.astype(grad_ref.dtype)
        sent_ref[:, lanes] = (cross_ref[...] * grad).astype(sent_ref.dtype)
        own_sum = own_sum + jnp.sum(pooled_ref[:, lanes].astype(F32) * grad, axis=0, keepdims=True)
        cross_sum = cross_sum + jnp.sum(partner_ref[:, lanes].astype(F32) * grad, axis=0, keepdims=True)
    for row, total in enumerate((own_sum, cross_sum)):
        folded = total[:, :width]
        for cell in range(1, reach // width):
            folded = folded + total[:, cell * width : (cell + 1) * width]
        sums_ref[row : row + 1, :] = folded


def join(here, far, pooled, partner_pool, cross_pool, target, core, block):
    slots, flat = pooled.shape
    count = flat // (4 * block)
    width = cross_pool.shape[0]
    if (4 * block) % 128:
        pieces = jnp.stack([jnp.stack([here[p][0], far[p]]) for p in range(count)])
        pieces = jnp.where(core == 0, pieces, pieces[:, ::-1]).reshape(count, 2, slots, 2, block)
        inverse = jnp.argsort(target)
        grad = jnp.take(pieces, inverse, axis=0).transpose(2, 0, 1, 3, 4).reshape(slots, flat)
        wide = grad.astype(F32)
        sent = (jnp.tile(cross_pool, flat // width) * wide).astype(BF16)
        sums = [
            jnp.sum(jnp.sum(a.astype(F32) * wide, axis=0).reshape(-1, width), axis=0) for a in (pooled, partner_pool)
        ]
        return grad, sent, jnp.stack(sums)
    smem = pl.BlockSpec(memory_space=pltpu.SMEM)
    vmem = pl.BlockSpec(memory_space=pltpu.VMEM)
    return pl.pallas_call(
        functools.partial(join_kernel, block, count, width),
        in_specs=[smem, smem] + [vmem] * (4 + count),
        out_specs=[vmem] * 3,
        out_shape=[
            jax.ShapeDtypeStruct((slots, flat), BF16),
            jax.ShapeDtypeStruct((slots, flat), BF16),
            jax.ShapeDtypeStruct((2, width), F32),
        ],
        compiler_params=pltpu.CompilerParams(vmem_limit_bytes=VMEM_LIMIT),
        cost_estimate=pl.CostEstimate(flops=0, bytes_accessed=0, transcendentals=0),
        name="join",
    )(target, core[None], jnp.tile(cross_pool, 4 * block // width)[None], pooled, partner_pool, far, *here)


def fc_forward_kernel(count, w_ref, got_ref, *refs):
    row_refs = refs[:count]
    chip_ref, sent_ref, all_ref = refs[count:]
    slots = got_ref.shape[1]

    @pl.when(pl.program_id(0) == 0)
    def _():
        for p in range(count):
            all_ref[pl.ds(p * slots, slots), :] = row_refs[p][0]
            all_ref[pl.ds((count + p) * slots, slots), :] = got_ref[p]

    total = jnp.dot(all_ref[...], w_ref[...], preferred_element_type=F32)
    half = count * slots
    for p in range(count):
        chip_ref[p] = total[p * slots : (p + 1) * slots]
        sent_ref[p] = total[half + p * slots : half + (p + 1) * slots].astype(sent_ref.dtype)


def fc_forward(rows, got, weight):
    count, (slots, depth), units = len(rows), got.shape[1:], weight.shape[1]
    tile = 1024
    if count > 4:
        used = jnp.concatenate([r[0] for r in rows] + [got.reshape(-1, depth)])
        total = jnp.dot(used, weight, preferred_element_type=F32).reshape(2, count, slots, units)
        return total[0], total[1].astype(BF16), used
    mine = pl.BlockSpec((1, slots, depth), lambda t: (0, 0, 0))
    out = pl.BlockSpec((count, slots, tile), lambda t: (0, 0, t))
    size = 2 * count * slots
    return pl.pallas_call(
        functools.partial(fc_forward_kernel, count),
        grid=(units // tile,),
        in_specs=[
            pl.BlockSpec((depth, tile), lambda t: (0, t)),
            pl.BlockSpec((count, slots, depth), lambda t: (0, 0, 0)),
        ]
        + [mine] * count,
        out_specs=[out, out, pl.BlockSpec((size, depth), lambda t: (0, 0))],
        out_shape=[
            jax.ShapeDtypeStruct((count, slots, units), F32),
            jax.ShapeDtypeStruct((count, slots, units), BF16),
            jax.ShapeDtypeStruct((size, depth), BF16),
        ],
        compiler_params=pltpu.CompilerParams(vmem_limit_bytes=VMEM_LIMIT),
        cost_estimate=pl.CostEstimate(flops=0, bytes_accessed=0, transcendentals=0),
        name="fc_forward",
    )(weight, got, *rows)


def fc_back_kernel(count, w_ref, own_ref, came_ref, *refs):
    out_refs, grads_ref = refs[:count], refs[count]
    slots, units = own_ref.shape[1:]
    half = count * slots

    @pl.when(pl.program_id(0) == 0)
    def _():
        grads_ref[:half] = own_ref[...].reshape(half, units)
        grads_ref[half:] = came_ref[...].reshape(half, units)

    total = lax.dot_general(grads_ref[...], w_ref[...], (((1,), (1,)), ((), ())), preferred_element_type=F32)
    for p, out_ref in enumerate(out_refs):
        for side in range(2):
            first = side * half + p * slots
            out_ref[side] = total[first : first + slots].astype(out_ref.dtype)


def fc_backward(own, came, weight):
    count, slots, units = own.shape
    depth = weight.shape[0]
    tile = 384 if depth % 384 == 0 else depth
    if count > 4:
        grads = jnp.stack([own, came], axis=1).reshape(-1, units)
        columns = lax.dot_general(grads, weight, (((1,), (1,)), ((), ())), preferred_element_type=F32)
        columns = columns.astype(BF16).reshape(count, 2, slots, depth)
        return [columns[p] for p in range(count)]
    grads = pl.BlockSpec((count, slots, units), lambda t: (0, 0, 0))
    return pl.pallas_call(
        functools.partial(fc_back_kernel, count),
        grid=(depth // tile,),
        in_specs=[pl.BlockSpec((tile, units), lambda t: (t, 0)), grads, grads],
        out_specs=[pl.BlockSpec((2, slots, tile), lambda t: (0, 0, t))] * count,
        out_shape=[jax.ShapeDtypeStruct((2, slots, depth), BF16)] * count,
        scratch_shapes=[pltpu.VMEM((2 * count * slots, units), BF16)],
        compiler_params=pltpu.CompilerParams(vmem_limit_bytes=VMEM_LIMIT),
        cost_estimate=pl.CostEstimate(flops=0, bytes_accessed=0, transcendentals=0),
        name="fc_backward",
    )(weight, own, came)


def halve_kernel(kept_ref, came_ref, out_ref, sent_ref):
    total = kept_ref[...] + came_ref[...].astype(F32)
    half = out_ref.shape[0]
    out_ref[...] = total[:half]
    sent_ref[...] = total[half:].astype(sent_ref.dtype)


def halve(kept, came):
    count, slots, units = kept.shape
    half = count // 2
    if count > 4:
        total = kept + came.astype(F32)
        return total[:half], total[half:].astype(BF16)
    tile = units // 4
    return pl.pallas_call(
        halve_kernel,
        grid=(4,),
        in_specs=[pl.BlockSpec((count, slots, tile), lambda t: (0, 0, t))] * 2,
        out_specs=[pl.BlockSpec((half, slots, tile), lambda t: (0, 0, t))] * 2,
        out_shape=[
            jax.ShapeDtypeStruct((half, slots, units), F32),
            jax.ShapeDtypeStruct((half, slots, units), BF16),
        ],
        compiler_params=pltpu.CompilerParams(vmem_limit_bytes=VMEM_LIMIT),
        cost_estimate=pl.CostEstimate(flops=0, bytes_accessed=0, transcendentals=0),
        name="halve",
    )(kept, came)


def hidden_kernel(kept_ref, came_ref, bias_ref, self_ref, cot_ref, scale_ref, back_ref, hidden_ref, grad_ref, sum_ref):
    pre = kept_ref[0] + came_ref[0].astype(F32) + bias_ref[...]
    hidden, slope = gelu_parts(pre)
    hidden_ref[...] = hidden.astype(hidden_ref.dtype)
    grad_out = cot_ref[...].astype(F32) * scale_ref[...]
    grad = ((self_ref[...] * grad_out + back_ref[...].astype(F32)) * slope).astype(grad_ref.dtype)
    grad_ref[0] = grad
    sum_ref[...] = jnp.sum(grad.astype(F32), axis=0, keepdims=True)


def hidden_step(n, kept, came, bias, self_fc, cotangent, scaling, back_fc):
    _, slots, units = kept.shape
    tile = units // 4
    one = pl.BlockSpec((1, tile), lambda t: (0, t))
    block = pl.BlockSpec((1, slots, tile), lambda t: (0, 0, t))
    rows = pl.BlockSpec((slots, tile), lambda t: (n, t))
    return pl.pallas_call(
        hidden_kernel,
        grid=(4,),
        in_specs=[block, block, one, one, rows, pl.BlockSpec((slots, 1), lambda t: (n, 0)), rows],
        out_specs=[pl.BlockSpec((slots, tile), lambda t: (0, t)), block, one],
        out_shape=[
            jax.ShapeDtypeStruct((slots, units), BF16),
            jax.ShapeDtypeStruct((1, slots, units), BF16),
            jax.ShapeDtypeStruct((1, units), F32),
        ],
        compiler_params=pltpu.CompilerParams(vmem_limit_bytes=VMEM_LIMIT),
        cost_estimate=pl.CostEstimate(flops=0, bytes_accessed=0, transcendentals=0),
        name="hidden",
    )(kept, came, bias[None], self_fc[None], cotangent, scaling[:, None], back_fc)


def unwritten(shape, dtype):
    return pl.pallas_call(
        lambda ref: None,
        out_specs=pl.BlockSpec(memory_space=pl.ANY),
        out_shape=jax.ShapeDtypeStruct(shape, dtype),
        cost_estimate=pl.CostEstimate(flops=0, bytes_accessed=0, transcendentals=0),
        name="unwritten",
    )()


def gelu_parts(v):
    root = 0.7978845608028654
    cubic = 0.044715
    square = v * v
    half = 0.5 + 0.5 * jnp.tanh(v * (root + (root * cubic) * square))
    slope = half + (half * (1.0 - half)) * (v * (2.0 * root + (6.0 * root * cubic) * square))
    return v * half, slope


def conv_forward(inputs, kernel, bias):
    pre_conv = lax.conv_general_dilated(
        inputs, kernel, (1, 1), ((1, 1), (1, 1)), dimension_numbers=CONV_DIMS, preferred_element_type=F32
    )
    activity, slope = gelu_parts(pre_conv + bias)
    e = jnp.exp(activity)
    return e.astype(BF16), ((0.5 * e) * slope).astype(BF16)


def conv_grad_inputs(grad_pre, kernel):
    turned = jnp.flip(kernel, (0, 1)).swapaxes(2, 3)
    return lax.conv_general_dilated(
        grad_pre, turned, (1, 1), ((1, 1), (1, 1)), dimension_numbers=CONV_DIMS, preferred_element_type=F32
    ).astype(BF16)


def conv_grad_kernel(inputs, grad_pre):
    dims = lax.ConvDimensionNumbers(lhs_spec=(3, 0, 1, 2), rhs_spec=(3, 0, 1, 2), out_spec=(2, 3, 0, 1))
    return lax.conv_general_dilated(
        inputs, grad_pre, (1, 1), ((1, 1), (1, 1)), dimension_numbers=dims, preferred_element_type=F32
    )


def sum_small(vector):
    vector = vector + swap_core(vector)
    vector = vector + swap_mid(vector)
    step = 1
    while step < lax.axis_size("outer"):
        vector = vector + swap_outer(vector, step)
        step *= 2
    return vector


def sum_kernel(stage, last, after, rows, outer, mid, core):
    outer_count = lax.axis_size("outer")
    for swap, side in ((swap_mid, mid), (swap_core, core)):
        halves = rows.reshape(2, -1, rows.shape[1])
        sent, kept = pick(halves, 1 - side).astype(BF16), pick(halves, side)
        last[0] = sent
        got = swap(sent)
        yield
        rows = kept + after(got).astype(F32)
    parts = rows.reshape(outer_count, -1, rows.shape[1])
    total = pick(parts, outer)
    sent = [pick(parts, outer ^ k).astype(BF16) for k in range(1, outer_count)]
    last[0] = sent[-1]
    got = [swap_outer(s, k + 1) for k, s in enumerate(sent)]
    yield
    got[0] = after(got[0])
    for g in got:
        total = total + g.astype(F32)
    total = total.astype(BF16)
    last[0] = total
    stack = [total] + [swap_outer(total, k) for k in range(1, outer_count)]
    yield
    stack = jnp.stack([after(total), *stack[1:]])
    rows = jnp.concatenate([pick(stack, outer ^ k) for k in range(outer_count)])
    for swap, side in ((swap_core, core), (swap_mid, mid)):
        last[0] = rows
        got = swap(rows)
        yield
        got = after(got)
        if swap is swap_mid:
            rows, got = rows.astype(F32), got.astype(F32)
        rows = jnp.where(side == 0, jnp.concatenate([rows, got]), jnp.concatenate([got, rows]))
    stage["kernel"] = rows


def body(
    features,
    conv_weight,
    conv_bias,
    fc_weight,
    fc_bias,
    stitch_pool,
    stitch_fc,
    cotangent,
    crop_counts,
    slot_image,
    slot_mask,
):
    is_first = lax.axis_index("tower") == 0
    core, mid, outer = lax.axis_index("core"), lax.axis_index("mid"), lax.axis_index("outer")
    outer_count = lax.axis_size("outer")
    block, units = fc_weight.shape[1:]
    weight = lax.all_gather(fc_weight[0], "mid", axis=0, tiled=True)

    row_pool = stitch_pool[0]
    self_pool = jnp.where(is_first, row_pool[0], row_pool[1])
    cross_pool = jnp.where(is_first, row_pool[1], row_pool[0])
    row_fc = stitch_fc[0]
    self_fc = jnp.where(is_first, row_fc[0], row_fc[1])
    cross_fc = jnp.where(is_first, row_fc[1], row_fc[0])

    live_slots = slot_mask.astype(F32)
    image_ids = jnp.arange(crop_counts.shape[0], dtype=jnp.int32)
    matches = (slot_image[:, None] == image_ids[None, :]).astype(F32)
    per_slot = jnp.sum(matches * crop_counts.astype(F32)[None, :], axis=1)
    scaling = live_slots / per_slot
    sent_fc = (cross_fc * (cotangent[0].astype(F32) * scaling[:, None])).astype(BF16)
    back_fc = swap_tower(sent_fc)

    inputs = features[0]
    kernel = conv_weight[0]
    width = kernel.shape[3]
    hops = outer_count.bit_length() - 1
    order = [sum(((p >> b) & 1) << (hops - 1 - b) for b in range(hops)) for p in range(outer_count)]
    target = outer ^ jnp.array(order, jnp.int32)
    total_slots = inputs.shape[0]
    sizes = [total_slots // 4] * 4 if outer_count <= 4 else [total_slots]
    starts = [sum(sizes[:n]) for n in range(len(sizes))]
    last = [scaling]

    def after(array):
        return lax.optimization_barrier((array, last[0]))[0]

    sums = dict(fc_bias=0.0, pool=0.0, conv_bias=0.0, kernel=0.0)
    stage = {}
    hiddens = {}
    count, extent, _, depth = inputs.shape
    stage["grad_in"] = jnp.transpose(unwritten((extent, extent, count, depth), BF16), (2, 0, 1, 3))
    lead = (((0,), (0,)), ((), ()))

    def chunk(n):
        slots = sizes[n]
        rows = slice(starts[n], starts[n] + slots)
        part = inputs[rows]
        e, slope = conv_forward(part, kernel, after(conv_bias[0]))
        pooled, inv = pool_forward(jnp.transpose(e, (1, 2, 0, 3)))
        last[0] = pooled
        partner_pool = swap_tower(pooled)
        yield
        rows_of = mix(after(pooled), partner_pool, self_pool, cross_pool, target, core, block)
        last[0] = rows_of[0]
        arrived = [rows_of[0]] + [swap_outer(r, k) for r, k in zip(rows_of[1:], order[1:])]
        yield
        arrived[0] = after(arrived[0])
        give = jnp.stack([r[1] for r in arrived])
        last[0] = give
        got = swap_core(give)
        yield
        chip, sent, flat = fc_forward(arrived, after(got), weight)
        last[0] = sent
        came = swap_core(sent)
        yield
        for hop in range(hops):
            chip, sent = halve(chip, after(came))
            last[0] = sent
            came = swap_outer(sent, 1 << hop)
            yield
        hiddens[n], gathered, bias_sum = hidden_step(
            n, chip, after(came), fc_bias[0], self_fc, cotangent[0], scaling, back_fc
        )
        sums["fc_bias"] += bias_sum[0]
        last[0] = gathered
        for hop in reversed(range(hops)):
            came = swap_outer(gathered, 1 << hop)
            yield
            gathered = jnp.concatenate([gathered, after(came)])
            last[0] = gathered
        came = swap_core(gathered)
        yield
        came = after(came)
        stage[n] = (flat, gathered, came)
        columns = fc_backward(gathered, came, weight)
        last[0] = columns[0]
        arrived = [columns[0]] + [swap_outer(c, k) for c, k in zip(columns[1:], order[1:])]
        yield
        arrived[0] = after(arrived[0])
        give = jnp.stack([r[1] for r in arrived])
        last[0] = give
        far = swap_core(give)
        yield
        grad_mixed, sent, stitch_sums = join(
            arrived, after(far), pooled, partner_pool, cross_pool, target, core, block
        )
        sums["pool"] += stitch_sums
        last[0] = sent
        back_pool = swap_tower(sent)
        yield
        grad_pre, bias_rows = pool_backward(
            jnp.transpose(slope, (1, 2, 0, 3)), grad_mixed, after(back_pool), inv, self_pool
        )
        sums["conv_bias"] += jnp.sum(bias_rows, axis=0)
        grad_pre = jnp.transpose(grad_pre, (2, 0, 1, 3))
        grad_kernel = conv_grad_kernel(part, grad_pre)
        sums["kernel"] += grad_kernel
        last[0] = grad_kernel
        yield
        part = conv_grad_inputs(after(grad_pre), kernel)
        stage["grad_in"] = lax.dynamic_update_slice(stage["grad_in"], part, (starts[n], 0, 0, 0))
        last[0] = stage["grad_in"]

    def stitch():
        hidden = after(jnp.concatenate([hiddens[n] for n in range(len(sizes))]))
        last[0] = hidden
        partner_hidden = swap_tower(hidden)
        yield
        partner_hidden = after(partner_hidden).astype(F32)
        hidden = hidden.astype(F32)
        stage["output"] = ((self_fc * hidden + cross_fc * partner_hidden) * live_slots[:, None]).astype(BF16)
        grad_out = cotangent[0].astype(F32) * scaling[:, None]
        stage["hidden"] = jnp.sum(hidden * grad_out, axis=0), jnp.sum(partner_hidden * grad_out, axis=0)
        last[0] = stage["output"]

    def fc_weight_gradient():
        columns = jnp.concatenate([stage[n][0] for n in range(len(sizes))])
        grads = after(jnp.concatenate([g.reshape(-1, units) for n in range(len(sizes)) for g in stage[n][1:]]))
        own, far = columns[:, :block], columns[:, block:]
        own, far = jnp.where(mid == 0, own, far), jnp.where(mid == 0, far, own)
        far_term = lax.dot_general(far, grads, lead, preferred_element_type=F32).astype(BF16)
        last[0] = far_term
        came = swap_mid(far_term)
        yield
        own, came = lax.optimization_barrier((own, after(came)))
        stage["gradient"] = lax.dot_general(own, grads, lead, preferred_element_type=F32) + came.astype(F32)
        last[0] = stage["gradient"]

    def kernel_sum():
        yield from sum_kernel(stage, last, after, sums["kernel"].reshape(-1, width), outer, mid, core)

    runs = {str(n): chunk(n) for n in range(len(sizes))}
    runs.update(W=fc_weight_gradient(), S=stitch(), A=kernel_sum())
    for n in "".join(PLAN) if len(sizes) > 1 else "0" * (2 * hops + 6) + "WS" + "0" * 4 + "AA0" + "WS" + "A" * 5:
        next(runs[n], None)
    grad_fc_weight = stage["gradient"]
    conv_bias_sum, fc_bias_sum = sums["conv_bias"], sums["fc_bias"]
    hidden_self, hidden_cross = stage["hidden"]
    pool_self, pool_cross = sums["pool"]

    small = sum_small(
        jnp.concatenate([conv_bias_sum, pool_self, pool_cross, fc_bias_sum, hidden_self, hidden_cross])[None]
    )[0]
    cuts = [width, 2 * width, 3 * width, 3 * width + units, 3 * width + 2 * units]
    conv_bias_sum, pool_self, pool_cross, fc_bias_sum, hidden_self, hidden_cross = jnp.split(small, cuts)
    grad_row_pool = jnp.where(
        is_first, jnp.stack([pool_self, pool_cross]), jnp.stack([pool_cross, pool_self])
    )
    grad_row_fc = jnp.where(
        is_first, jnp.stack([hidden_self, hidden_cross]), jnp.stack([hidden_cross, hidden_self])
    )
    summed_kernel = stage["kernel"].reshape(kernel.shape)
    return (
        stage["output"][None],
        stage["grad_in"][None],
        summed_kernel[None],
        conv_bias_sum[None],
        grad_fc_weight[None],
        fc_bias_sum[None],
        grad_row_pool[None],
        grad_row_fc[None],
    )


def solution(mesh):
    mesh = jax.sharding.Mesh(mesh.devices.reshape(mesh.shape["tower"], -1, 2, 2), ("tower", "outer", "core", "mid"))
    crops = ("outer", "core", "mid")
    placed = (
        P("tower", crops, None, None, None),
        P("tower", None, None, None, None),
        P("tower", None),
        P("tower", crops, None),
        P("tower", None),
        P("tower", None, None),
        P("tower", None, None),
        P("tower", crops, None),
        P(crops),
        P(crops),
        P(crops),
    )
    return jax.shard_map(
        body,
        mesh=mesh,
        in_specs=placed,
        out_specs=(
            P("tower", crops, None),
            P("tower", crops, None, None, None),
            P("tower", None, None, None, None),
            P("tower", None),
            P("tower", crops, None),
            P("tower", None),
            P("tower", None, None),
            P("tower", None, None),
        ),
        check_vma=False,
    )
```
